256 devices in a mesh: pair: 32 (over x, y, core), win: 8 (over z).
Axes of the slice: x: 4, y: 4, z: 8, core: 2. Of those that a mesh axis runs over, the one named last changes fastest.
Arguments:
- spectra: bfloat16 [16, 2048, 2, 2048], P('win', 'pair')
- passband: float32 [2048], replicated, may hold values from 0.1 to 1
- pair_ends: int32 [32, 128, 2], replicated, may hold values from 0 to 2047, as said below
- live_pairs: int32 [32], P('pair'), may hold values from 32 to 128, as said below
Outputs:
- stacked: float32 [4096, 4096], P('pair', 'win')
The draws below stay inside these ranges and needn't reach their ends.
Inputs may be any that keep to these rules, and one draw needn't show every extreme that they name: `pair_ends`: entries are channel numbers. The first channel of every slot of block b lies in b * 64 to (b + 1) * 64 - 1; the second lies in the channels of blocks b - 3 to b + 3, and in every block some second channel lies exactly 3 blocks away. How many second channels fall on each nearby block varies. `live_pairs`: some block uses all its slots and some block uses 128 // 4.
All inputs are finite; a program needn't handle non-finite values. Where the reference program divides by a largest or mean magnitude, that divisor is 1e-20 or more.
Results may differ from the reference program's by a relative error of at most 0.0057.
Values may be sent and summed in bfloat16 or wider, within the bound.
No kernel may reach another device: no remote copies, remote signals or barrier semaphores. Data moves between devices by JAX's collectives and lax.ppermute only.
A program may use at most 64 MiB of HBM per device.

```python
import math
import jax
import jax.numpy as jnp
from jax import lax

BINS = 2048
LAGS = 4096
HALF = 3
CH_DEV = 64
CHANNELS = 2048
WINDOWS = 16
P_BLK = 128
N_PAIR = 32


def draw_spectra(key, part):
    key = jax.random.fold_in(key, 3)
    key_base, key_rows, key_bins = jax.random.split(key, 3)
    base = jax.random.normal(key_base, (WINDOWS, CHANNELS, 2, BINS), jnp.float32)
    row_scale = jnp.exp(jax.random.uniform(key_rows, (WINDOWS, CHANNELS, 1, 1), jnp.float32, 0.0, math.log(10.0)))
    bin_scale = jnp.exp(jax.random.uniform(key_bins, (WINDOWS, CHANNELS, 1, BINS), jnp.float32, math.log(0.5), math.log(2.0)))
    return (base * row_scale * bin_scale).astype(jnp.bfloat16)


def draw_pair_ends(key, part):
    key = jax.random.fold_in(key, 1)
    key_first, key_weight, key_pick, key_second = jax.random.split(key, 4)
    blocks = jnp.arange(N_PAIR, dtype=jnp.int32)[:, None]
    first = blocks * CH_DEV + jax.random.randint(key_first, (N_PAIR, P_BLK), 0, CH_DEV, dtype=jnp.int32)
    weights = jax.random.randint(key_weight, (N_PAIR, 2 * HALF + 1), 1, 9, dtype=jnp.int32)
    running = jnp.cumsum(weights, axis=1).astype(jnp.int32)
    picks = jax.random.randint(key_pick, (N_PAIR, P_BLK), 0, 1 << 20, dtype=jnp.int32) % running[:, -1:]
    offset = jnp.sum((picks[:, :, None] >= running[:, None, :]).astype(jnp.int32), axis=2).astype(jnp.int32) - HALF
    forced = jnp.where(blocks[:, 0] + HALF < N_PAIR, HALF, -HALF).astype(jnp.int32)
    offset = offset.at[:, 0].set(forced)
    owner = blocks + offset
    owner = jnp.where(owner < 0, -owner, owner)
    owner = jnp.where(owner >= N_PAIR, 2 * (N_PAIR - 1) - owner, owner)
    second = owner * CH_DEV + jax.random.randint(key_second, (N_PAIR, P_BLK), 0, CH_DEV, dtype=jnp.int32)
    return jnp.stack([first, second], axis=2).astype(jnp.int32)


def draw_live_pairs(key, part):
    key = jax.random.fold_in(key, 2)
    key_vals, key_top, key_low = jax.random.split(key, 3)
    counts = jax.random.randint(key_vals, (N_PAIR,), P_BLK // 4, P_BLK + 1, dtype=jnp.int32)
    top_block = jax.random.randint(key_top, (), 0, N_PAIR, dtype=jnp.int32)
    low_block = (top_block + 1 + jax.random.randint(key_low, (), 0, N_PAIR - 1, dtype=jnp.int32)) % N_PAIR
    counts = counts.at[top_block].set(P_BLK)
    counts = counts.at[low_block].set(P_BLK // 4)
    return counts.astype(jnp.int32)


def setup_inputs(seed: int = 0) -> dict:
    key_list = jax.random.split(jax.random.key(seed), 5)
    spectra = draw_spectra(jax.random.fold_in(key_list[4], 71), 0)
    passband = jnp.clip(jnp.exp(jax.random.uniform(key_list[1], (BINS,), jnp.float32, math.log(0.1), math.log(1.0))), 0.1, 1.0)
    pair_ends = draw_pair_ends(jax.random.fold_in(key_list[4], 71), 0)
    live_pairs = draw_live_pairs(jax.random.fold_in(key_list[4], 71), 0)
    return dict(spectra=spectra, passband=passband, pair_ends=pair_ends, live_pairs=live_pairs)


def whiten(spectra):
    values = spectra.astype(jnp.float32)
    power = lax.optimization_barrier(jnp.mean(values * values, axis=(2, 3), keepdims=True))
    return (values * lax.rsqrt(power + 1e-06)).astype(jnp.bfloat16)

def cross_spectra(endpoints, passband, live_mask):
    win_count = endpoints.shape[0]
    pair_count = endpoints.shape[1] // 2
    bin_count = endpoints.shape[3]
    split_ends = endpoints.reshape(win_count, pair_count, 2, 2, bin_count).astype(jnp.float32)
    first_end = split_ends[:, :, 0]
    second_end = split_ends[:, :, 1]
    weighting = passband[None, None, :] * live_mask[None, :, None]
    real_part = (first_end[:, :, 0] * second_end[:, :, 0] + first_end[:, :, 1] * second_end[:, :, 1]) * weighting
    imag_part = (first_end[:, :, 1] * second_end[:, :, 0] - first_end[:, :, 0] * second_end[:, :, 1]) * weighting
    return jnp.concatenate([real_part, imag_part], axis=2).astype(jnp.bfloat16)

def lag_table(bin_count, lag_start, lag_count):
    lag_total = 2 * bin_count
    freqs = jnp.arange(bin_count, dtype=jnp.int32)
    lag_index = lag_start + jnp.arange(lag_count, dtype=jnp.int32)
    phases = freqs[:, None] * lag_index[None, :] % lag_total
    angles = phases.astype(jnp.float32) * (2.0 * math.pi / lag_total)
    factor = jnp.where(freqs == 0, 1.0, 2.0).astype(jnp.float32)[:, None]
    return jnp.concatenate([factor * jnp.cos(angles), -factor * jnp.sin(angles)], axis=0).astype(jnp.bfloat16)

def reference(spectra, passband, pair_ends, live_pairs):
    whitened = whiten(spectra)
    slot_count = pair_ends.shape[1]
    lag_cols = lax.optimization_barrier(lag_table(BINS, 0, LAGS)).astype(jnp.float32)

    def one_block(inputs):
        block_ends, live_count = inputs
        endpoints = jnp.take(whitened, block_ends.reshape(-1).astype(jnp.int32), axis=1)
        live_mask = (jnp.arange(slot_count, dtype=jnp.int32) < live_count).astype(jnp.float32)
        cross_spec = cross_spectra(endpoints, passband, live_mask)
        corr = jnp.dot(cross_spec.reshape(-1, 2 * BINS).astype(jnp.float32), lag_cols, precision=lax.Precision.HIGHEST, preferred_element_type=jnp.float32)
        peak = lax.optimization_barrier(jnp.max(jnp.abs(corr), axis=1, keepdims=True)) + 1e-06
        return lax.optimization_barrier(jnp.sum((corr / peak).reshape(WINDOWS, slot_count, LAGS), axis=0))
    summed = lax.map(one_block, (pair_ends, live_pairs))
    return summed.reshape(-1, LAGS) * (1.0 / math.sqrt(WINDOWS))
```

```python
import functools
import math

import jax
import jax.numpy as jnp
from jax import lax
from jax.experimental import pallas as pl
from jax.experimental.pallas import tpu as pltpu
from jax.sharding import PartitionSpec as P

HALF = 3
BF = jnp.bfloat16
F32 = jnp.float32
VM = pl.BlockSpec(memory_space=pltpu.VMEM)
SM = pl.BlockSpec(memory_space=pltpu.SMEM)
ANY = pl.BlockSpec(memory_space=pl.ANY)

LANES = 128
SUBS = 16
LOW = 2 * SUBS
GROUP = 8


def shift(value, steps):
    count = lax.axis_size("pair")
    return lax.ppermute(
        value, "pair", [(i, i + steps) for i in range(max(0, -steps), min(count, count - steps))]
    )


def swap(value):
    count = lax.axis_size("pair")
    return lax.ppermute(value, "pair", [(i, i ^ 1) for i in range(count)])


def outward(value):
    count = lax.axis_size("pair")
    pairs = [(i, i - 1 if i % 2 == 0 else i + 1) for i in range(count)]
    return lax.ppermute(value, "pair", [(a, b) for a, b in pairs if 0 <= b < count])


def whiten_kernel(perm_ref, x_ref, *out_refs):
    rows = 2 * SUBS
    for window, out_ref in enumerate(out_refs):
        def step(c, _, window=window, out_ref=out_ref):
            values = x_ref[window, pl.ds(c * GROUP, GROUP)].astype(F32)
            power = jnp.mean(jnp.mean(values * values, axis=2, keepdims=True), axis=1, keepdims=True)
            scaled = (values * lax.rsqrt(power + 1e-06)).astype(BF)
            flat = scaled.reshape(GROUP * rows, LANES)
            ordered = jnp.dot(perm_ref[...], flat, preferred_element_type=F32)
            out_ref[pl.ds(c * GROUP, GROUP)] = ordered.astype(BF).reshape(GROUP, rows, LANES)
            return 0

        lax.fori_loop(0, x_ref.shape[1] // GROUP, step, 0)


def corr_kernel(last, first_ref, second_ref, live_ref, *refs):
    near_refs, refs = refs[:7], refs[7:]
    weight_ref, fold_ref, wave_ref, *refs = refs
    prev_ref = None
    if last:
        prev_ref, *refs = refs
    out_ref, near, cross, mid, corr, sem = refs
    channels = near_refs[0].shape[0]
    slots = mid.shape[1]
    for n, ref in enumerate(near_refs):
        pltpu.make_async_copy(ref, near.at[pl.ds(n * channels, channels)], sem.at[n]).start()
    for n, ref in enumerate(near_refs):
        pltpu.make_async_copy(ref, near.at[pl.ds(n * channels, channels)], sem.at[n]).wait()
    weight = weight_ref[...]
    for g in range(slots // (2 * GROUP)):
        buf = g % 2
        for half in range(2):
            for q in range(GROUP):
                p = g * 2 * GROUP + half * GROUP + q
                a = near[first_ref[p]].astype(F32)
                b = near[second_ref[p]].astype(F32)
                ar, ai, br, bi = a[:SUBS], a[SUBS:], b[:SUBS], b[SUBS:]
                re = (ar * br + ai * bi) * weight
                im = (ai * br - ar * bi) * weight
                at = pl.ds(half * LANES, LANES)
                cross[buf, pl.ds(q * 2 * SUBS, SUBS), at] = re.astype(BF)
                cross[buf, pl.ds(q * 2 * SUBS + SUBS, SUBS), at] = im.astype(BF)
        y = jnp.dot(fold_ref[...], cross[buf], preferred_element_type=F32)
        for part in range(2):
            z = y[part * LOW * GROUP : (part + 1) * LOW * GROUP]
            z = jnp.concatenate(
                [
                    z[:, :LANES].reshape(LOW, GROUP, LANES),
                    z[:, LANES:].reshape(LOW, GROUP, LANES),
                ],
                axis=1,
            )
            mid[:, pl.ds(g * 2 * GROUP, 2 * GROUP), pl.ds(part * LANES, LANES)] = z.astype(BF)

    def lags(t2, top):
        c = lax.dot_general(
            wave_ref[t2], mid[t2], (((1,), (1,)), ((), ())), preferred_element_type=F32
        )
        corr[t2] = c
        return jnp.maximum(top, jnp.abs(c))

    top = lax.fori_loop(0, LOW, lags, jnp.zeros((LANES, slots), F32), unroll=4)
    peak = jnp.max(top, axis=0, keepdims=True) + 1e-06
    alive = lax.broadcasted_iota(jnp.int32, (1, slots), 1) < live_ref[0]
    scale = jnp.where(alive, 0.25 / peak, 0.0)
    parts = out_ref.shape[0]
    wide = LANES // parts

    def emit(t2, _):
        for z in range(parts):
            c = corr[t2, pl.ds(z * wide, wide)] * scale
            if last:
                c = c + prev_ref[z, t2]
            out_ref[z, t2] = c.astype(out_ref.dtype)
        return 0

    lax.fori_loop(0, LOW, emit, 0, unroll=2)


def final_kernel(x_ref, out_ref):
    low, wide, slots = x_ref.shape
    rows = jnp.concatenate([x_ref[:, t, :] for t in range(wide)], axis=0)
    out_ref[...] = rows.astype(F32).T


def tables():
    i32 = jnp.int32
    lags = LOW * LANES
    row = jnp.arange(2 * LOW * GROUP, dtype=i32)[:, None]
    col = jnp.arange(2 * SUBS * GROUP, dtype=i32)[None, :]
    out_part, t2, q_row = row // (LOW * GROUP), (row // GROUP) % LOW, row % GROUP
    q_col, in_part, s = col // (2 * SUBS), (col // SUBS) % 2, col % SUBS
    angle = ((s * t2) % LOW).astype(F32) * (2.0 * math.pi / LOW)
    same = jnp.cos(angle)
    cross = jnp.where(out_part == 0, -jnp.sin(angle), jnp.sin(angle))
    fold = jnp.where(out_part == in_part, same, cross)
    fold = jnp.where(q_row == q_col, fold, 0.0).astype(BF)
    t = jnp.arange(LOW, dtype=i32)[:, None, None] + LOW * jnp.arange(LANES, dtype=i32)[None, :, None]
    l = jnp.arange(LANES, dtype=i32)[None, None, :]
    angle = ((l * t) % lags).astype(F32) * (2.0 * math.pi / lags)
    wave = jnp.concatenate([jnp.cos(angle), -jnp.sin(angle)], axis=2).astype(BF)
    return fold, wave


def local(spectra, passband, pair_ends, live_pairs):
    win_count = lax.axis_size("win")
    win_dev, ch_dev, _, bins = spectra.shape
    slots = pair_ends.shape[1]
    rows = 2 * SUBS
    x = spectra.reshape(win_dev, ch_dev, 2, SUBS, LANES).transpose(0, 1, 3, 2, 4)
    x = x.reshape(win_dev, ch_dev, rows, LANES)
    r = jnp.arange(GROUP * rows, dtype=jnp.int32)
    source = (r // rows) * rows + 2 * (r % SUBS) + (r // SUBS) % 2
    perm = (source[:, None] == r[None, :]).astype(BF)
    whitened = pl.pallas_call(
        whiten_kernel,
        out_shape=[jax.ShapeDtypeStruct((ch_dev, rows, LANES), BF)] * win_dev,
        in_specs=[VM, VM],
        out_specs=[VM] * win_dev,
        compiler_params=pltpu.CompilerParams(vmem_limit_bytes=16 << 20),
    )(perm, x)

    me = lax.axis_index("pair")
    odd = me % 2
    near = []
    for w in whitened:
        up, down = shift(w, -2), shift(w, 2)
        near.append([w, swap(w), up, down])
    for n in near:
        n.extend([swap(n[2]), swap(n[3]), outward(jnp.where(odd == 0, n[2], n[3]))])

    ends = lax.dynamic_index_in_dim(pair_ends, me, 0, keepdims=False)
    first = ends[:, 0] % ch_dev
    away = ends[:, 1] // ch_dev - me
    even_at = {0: 0, 1: 1, 2: 2, -2: 3, 3: 4, -1: 5, -3: 6}
    odd_at = {0: 0, -1: 1, 2: 2, -2: 3, 1: 4, -3: 5, 3: 6}
    place = jnp.zeros_like(away)
    for d in range(-HALF, HALF + 1):
        place = jnp.where(away == d, jnp.where(odd == 0, even_at[d], odd_at[d]), place)
    second = place * ch_dev + ends[:, 1] % ch_dev

    fold, wave = tables()
    factor = jnp.where(jnp.arange(bins) == 0, 1.0, 2.0).astype(F32)
    weight = (passband * factor).reshape(SUBS, LANES)

    total = None
    for v in range(win_dev):
        last = v == win_dev - 1
        args = [first, second, live_pairs, *near[v], weight, fold, wave]
        specs = [SM, SM, SM] + [ANY] * 7 + [VM, VM, VM]
        if last:
            args.append(total)
            specs.append(VM)
        total = pl.pallas_call(
            functools.partial(corr_kernel, last),
            out_shape=jax.ShapeDtypeStruct(
                (win_count, LOW, LANES // win_count, slots), BF if last else F32
            ),
            in_specs=specs,
            out_specs=VM,
            scratch_shapes=[
                pltpu.VMEM((7 * ch_dev, rows, LANES), BF),
                pltpu.VMEM((2, GROUP * rows, 2 * LANES), BF),
                pltpu.VMEM((LOW, slots, 2 * LANES), BF),
                pltpu.VMEM((LOW, LANES, slots), F32),
                pltpu.SemaphoreType.DMA((7,)),
            ],
            compiler_params=pltpu.CompilerParams(vmem_limit_bytes=40 << 20),
            cost_estimate=pl.CostEstimate(
                flops=2 * slots * 64 * 4096, bytes_accessed=8 << 20, transcendentals=0
            ),
        )(*args)

    mine = lax.psum_scatter(total, "win", scatter_dimension=0, tiled=True)[0]
    return pl.pallas_call(
        final_kernel,
        out_shape=jax.ShapeDtypeStruct((slots, LOW * LANES // win_count), F32),
        in_specs=[VM],
        out_specs=VM,
    )(mine)


def solution(mesh):
    placed = (P("win", "pair", None, None), P(), P(), P("pair"))
    return jax.shard_map(
        local, mesh=mesh, in_specs=placed, out_specs=P("pair", "win"), check_vma=False
    )
```

```python
import functools
import math

import jax
import jax.numpy as jnp
from jax import lax
from jax.experimental import pallas as pl
from jax.experimental.pallas import tpu as pltpu
from jax.sharding import PartitionSpec as P

HALF = 3
BF = jnp.bfloat16
F32 = jnp.float32
VM = pl.BlockSpec(memory_space=pltpu.VMEM)
SM = pl.BlockSpec(memory_space=pltpu.SMEM)
ANY = pl.BlockSpec(memory_space=pl.ANY)

LANES = 128
SUBS = 16
LOW = 2 * SUBS
GROUP = 8


def moved(value, where):
    count = lax.axis_size("pair")
    pairs = [(i, where(i)) for i in range(count)]
    return lax.ppermute(value, "pair", [(a, b) for a, b in pairs if 0 <= b < count])


def swap(value):
    count = lax.axis_size("pair")
    return lax.ppermute(value, "pair", [(i, i ^ 1) for i in range(count)])


def whiten_kernel(x_ref, out_ref):
    rows = 2 * SUBS
    size = GROUP * rows
    r = lax.broadcasted_iota(jnp.int32, (size, size), 0)
    c = lax.broadcasted_iota(jnp.int32, (size, size), 1)
    source = (r // rows) * rows + 2 * (r % SUBS) + (r // SUBS) % 2
    perm = jnp.where(c == source, 1.0, 0.0).astype(BF)

    for window in range(x_ref.shape[0]):
        for g in range(x_ref.shape[1] // GROUP):
            at = pl.ds(g * GROUP, GROUP)
            values = x_ref[window, at].astype(F32)
            power = jnp.sum(jnp.sum(values * values, axis=1), axis=1, keepdims=True)
            power = power * (1.0 / (rows * LANES))
            scaled = (values * lax.rsqrt(power + 1e-06)[:, :, None]).astype(BF)
            ordered = jnp.dot(perm, scaled.reshape(size, LANES), preferred_element_type=F32)
            out_ref[window, at] = ordered.astype(BF).reshape(GROUP, rows, LANES)


def stage_kernel(*refs):
    *near_refs, out_ref, sem = refs
    channels = near_refs[0].shape[1]
    copies = [
        pltpu.make_async_copy(
            ref.at[v], out_ref.at[v, pl.ds(n * channels, channels)], sem.at[n, v]
        )
        for n, ref in enumerate(near_refs)
        for v in range(ref.shape[0])
    ]
    for copy in copies:
        copy.start()
    for copy in copies:
        copy.wait()


def corr_kernel(
    first_ref,
    second_ref,
    live_ref,
    z_ref,
    near_ref,
    weight_ref,
    fold_ref,
    wave_ref,
    keep_ref,
    up_ref,
    down_ref,
    cross,
    mid,
    corr,
):
    windows = near_ref.shape[0]
    slots = mid.shape[1] // windows
    weight = weight_ref[...]
    alive = lax.broadcasted_iota(jnp.int32, (1, slots), 1) < live_ref[0]
    _, half_rows, wide, _ = up_ref.shape
    count = LANES // wide

    for v in range(windows):
        for g in range(slots // (2 * GROUP)):
            buf = g % 2
            for half in range(2):
                for q in range(GROUP):
                    p = g * 2 * GROUP + half * GROUP + q
                    a = near_ref[v, first_ref[p]].astype(F32)
                    b = near_ref[v, second_ref[p]].astype(F32)
                    ar, ai, br, bi = a[:SUBS], a[SUBS:], b[:SUBS], b[SUBS:]
                    re = (ar * br + ai * bi) * weight
                    im = (ai * br - ar * bi) * weight
                    cols = pl.ds(half * LANES, LANES)
                    cross[buf, pl.ds(q * 2 * SUBS, SUBS), cols] = re.astype(BF)
                    cross[buf, pl.ds(q * 2 * SUBS + SUBS, SUBS), cols] = im.astype(BF)
            y = jnp.dot(fold_ref[...], cross[buf], preferred_element_type=F32)
            for part in range(2):
                z = y[part * LOW * GROUP : (part + 1) * LOW * GROUP]
                z = jnp.concatenate(
                    [
                        z[:, :LANES].reshape(LOW, GROUP, LANES),
                        z[:, LANES:].reshape(LOW, GROUP, LANES),
                    ],
                    axis=1,
                )
                rows = pl.ds(v * slots + g * 2 * GROUP, 2 * GROUP)
                mid[:, rows, pl.ds(part * LANES, LANES)] = z.astype(BF)

    def lags(t2, top):
        c = lax.dot_general(
            wave_ref[t2], mid[t2], (((1,), (1,)), ((), ())), preferred_element_type=F32
        )
        corr[t2] = c
        return jnp.maximum(top, jnp.abs(c))

    top = jnp.zeros((LANES, windows * slots), F32)
    top = lax.fori_loop(0, LOW, lags, top, unroll=True)
    peak = jnp.max(top, axis=0, keepdims=True) + 1e-06
    scale = [
        jnp.where(alive, 0.25 / peak[:, v * slots : (v + 1) * slots], 0.0)
        for v in range(windows)
    ]

    jobs = []
    for step, give_ref in ((1, up_ref), (-1, down_ref)):
        jobs += [(step, n, give_ref, n) for n in range(2)]
        jobs += [(-2 * step, n, give_ref, 2 + n) for n in range(2)]
        jobs += [(4, (1 + step) // 2, give_ref, 4)]
    for k, step in enumerate((0, -3, 3)):
        jobs += [(step, n, keep_ref, 2 * k + n) for n in range(2)]
    for step, n, ref, at in jobs:
        rows = pl.ds(lax.rem(z_ref[0] + step + count, count) * wide, wide)

        def emit(t, _, n=n, ref=ref, at=at, rows=rows):
            t2 = t + n * half_rows
            value = corr[t2, rows, pl.ds(0, slots)] * scale[0]
            for v in range(1, windows):
                value = value + corr[t2, rows, pl.ds(v * slots, slots)] * scale[v]
            ref[at, t] = value.astype(ref.dtype)
            return 0

        lax.fori_loop(0, half_rows, emit, 0, unroll=True)


def merge_kernel(keep_ref, left_ref, right_ref, own_ref, behind_ref, ahead_ref):
    for n in range(2):
        own_ref[n] = keep_ref[n] + left_ref[n].astype(F32) + right_ref[n].astype(F32)
        behind = keep_ref[2 + n] + left_ref[2 + n].astype(F32)
        ahead = keep_ref[4 + n] + right_ref[2 + n].astype(F32)
        if n == 0:
            behind = behind + right_ref[4].astype(F32)
        else:
            ahead = ahead + left_ref[4].astype(F32)
        behind_ref[n] = behind.astype(BF)
        ahead_ref[n] = ahead.astype(BF)


def final_kernel(own_ref, *refs):
    *other_refs, out_ref, total = refs
    halves, half_rows, wide, _ = own_ref.shape
    low = halves * half_rows
    for t2 in range(low):
        n, t = divmod(t2, half_rows)
        rows = own_ref[n, t]
        for ref in other_refs:
            rows = rows + ref[n, t].astype(F32)
        total[pl.ds(t2 * wide, wide)] = rows
    group = LANES // low
    for g in range(wide // group):
        rows = [total[pl.ds(g * group + t, low, stride=wide)] for t in range(group)]
        out_ref[:, pl.ds(g * LANES, LANES)] = jnp.concatenate(rows, axis=0).T


def table_kernel(own_ref, _, fold_ref, wave_ref, again_ref):
    def turns(rows, cols, period):
        r = lax.broadcasted_iota(jnp.int32, (rows, cols), 0)
        c = lax.broadcasted_iota(jnp.int32, (rows, cols), 1)
        angle = lax.rem(r * c, period).astype(F32) * (2.0 * math.pi / period)
        return jnp.cos(angle), jnp.sin(angle)

    again_ref[...] = own_ref[...]

    cos, sin = turns(LOW, SUBS, LOW)
    base = jnp.concatenate(
        [jnp.concatenate([cos, -sin], axis=1), jnp.concatenate([sin, cos], axis=1)], axis=0
    ).astype(BF)
    rows, cols = fold_ref.shape
    spread_rows = lax.broadcasted_iota(jnp.int32, (rows, 2 * LOW), 0) // GROUP
    spread_rows = spread_rows == lax.broadcasted_iota(jnp.int32, (rows, 2 * LOW), 1)
    spread_cols = lax.rem(lax.broadcasted_iota(jnp.int32, (2 * SUBS, cols), 1), 2 * SUBS)
    spread_cols = spread_cols == lax.broadcasted_iota(jnp.int32, (2 * SUBS, cols), 0)
    fold = jnp.dot(spread_rows.astype(F32).astype(BF), base, preferred_element_type=F32)
    fold = jnp.dot(
        fold.astype(BF), spread_cols.astype(F32).astype(BF), preferred_element_type=F32
    )
    q_row = lax.rem(lax.broadcasted_iota(jnp.int32, (rows, cols), 0), GROUP)
    q_col = lax.broadcasted_iota(jnp.int32, (rows, cols), 1) // (2 * SUBS)
    fold_ref[...] = jnp.where(q_row == q_col, fold, 0.0).astype(BF)

    low_cos, low_sin = turns(LOW, LANES, LOW * LANES)
    high_cos, high_sin = turns(LANES, LANES, LANES)
    for t2 in range(LOW):
        c, s = low_cos[t2 : t2 + 1], low_sin[t2 : t2 + 1]
        wave_ref[t2, :, pl.ds(0, LANES)] = (c * high_cos - s * high_sin).astype(BF)
        wave_ref[t2, :, pl.ds(LANES, LANES)] = (-s * high_cos - c * high_sin).astype(BF)


def local(spectra, passband, pair_ends, live_pairs):
    win_count = lax.axis_size("win")
    win_dev, ch_dev, _, bins = spectra.shape
    slots = pair_ends.shape[1]
    rows = 2 * SUBS
    wide = LANES // win_count
    half = LOW // 2
    x = spectra.reshape(win_dev, ch_dev, 2, SUBS, LANES).transpose(0, 1, 3, 2, 4)
    x = x.reshape(win_dev, ch_dev, rows, LANES)
    own = pl.pallas_call(
        whiten_kernel,
        out_shape=jax.ShapeDtypeStruct(x.shape, BF),
        in_specs=[VM],
        out_specs=VM,
        compiler_params=pltpu.CompilerParams(vmem_limit_bytes=16 << 20),
    )(x)
    me = lax.axis_index("pair")
    odd = me % 2
    ahead = moved(own, lambda i: i - 2 if i % 2 == 0 else i + 2)
    sib = swap(own)
    fold, wave, again = pl.pallas_call(
        table_kernel,
        out_shape=[
            jax.ShapeDtypeStruct((2 * LOW * GROUP, 2 * SUBS * GROUP), BF),
            jax.ShapeDtypeStruct((LOW, LANES, 2 * LANES), BF),
            jax.ShapeDtypeStruct(own.shape, BF),
        ],
        in_specs=[VM, ANY],
        out_specs=[VM] * 3,
        compiler_params=pltpu.CompilerParams(vmem_limit_bytes=16 << 20),
        cost_estimate=pl.CostEstimate(
            flops=1 << 30, bytes_accessed=2 << 20, transcendentals=0
        ),
    )(own, sib)
    back = moved(again, lambda i: i + 2 if i % 2 == 0 else i - 2)
    far = moved(ahead, lambda i: i - 1 if i % 2 == 0 else i + 1)
    near = [own, sib, ahead, swap(ahead), back, swap(back), far]
    near = pl.pallas_call(
        stage_kernel,
        out_shape=jax.ShapeDtypeStruct((win_dev, len(near) * ch_dev, rows, LANES), BF),
        in_specs=[ANY] * len(near),
        out_specs=VM,
        scratch_shapes=[pltpu.SemaphoreType.DMA((len(near), win_dev))],
        compiler_params=pltpu.CompilerParams(vmem_limit_bytes=32 << 20),
        cost_estimate=pl.CostEstimate(
            flops=1 << 30, bytes_accessed=8 << 20, transcendentals=0
        ),
    )(*near)

    ends = lax.dynamic_index_in_dim(pair_ends, me, 0, keepdims=False)
    first = ends[:, 0] % ch_dev
    away = (ends[:, 1] // ch_dev - me) * (1 - 2 * odd)
    place = jnp.zeros_like(away)
    for n, d in enumerate((0, 1, 2, -1, -2, 3, -3)):
        place = jnp.where(away == d, n, place)
    second = place * ch_dev + ends[:, 1] % ch_dev

    factor = jnp.where(jnp.arange(bins) == 0, 1.0, 2.0).astype(F32)
    weight = (passband * factor).reshape(SUBS, LANES)

    z = lax.axis_index("win")
    give = jax.ShapeDtypeStruct((5, half, wide, slots), BF)
    keep, up, down = pl.pallas_call(
        corr_kernel,
        out_shape=[jax.ShapeDtypeStruct((6, half, wide, slots), F32), give, give],
        in_specs=[SM] * 4 + [VM] * 4,
        out_specs=[VM] * 3,
        scratch_shapes=[
            pltpu.VMEM((2, GROUP * rows, 2 * LANES), BF),
            pltpu.VMEM((LOW, win_dev * slots, 2 * LANES), BF),
            pltpu.VMEM((LOW, LANES, win_dev * slots), F32),
        ],
        compiler_params=pltpu.CompilerParams(vmem_limit_bytes=32 << 20),
        cost_estimate=pl.CostEstimate(
            flops=8 << 30, bytes_accessed=8 << 20, transcendentals=0
        ),
    )(first, second, live_pairs, z.reshape(1), near, weight, fold, wave)

    def along(value, step):
        return lax.ppermute(
            value, "win", [(i, (i + step) % win_count) for i in range(win_count)]
        )

    piece = (2, half, wide, slots)
    mine, behind, ahead = pl.pallas_call(
        merge_kernel,
        out_shape=[jax.ShapeDtypeStruct(piece, d) for d in (F32, BF, BF)],
        in_specs=[VM] * 3,
        out_specs=[VM] * 3,
        compiler_params=pltpu.CompilerParams(vmem_limit_bytes=16 << 20),
    )(keep, along(up, 1), along(down, -1))
    return pl.pallas_call(
        final_kernel,
        out_shape=jax.ShapeDtypeStruct((slots, LOW * wide), F32),
        in_specs=[VM] * 3,
        out_specs=VM,
        scratch_shapes=[pltpu.VMEM((LOW * wide, slots), F32)],
    )(mine, along(behind, -3), along(ahead, 3))


def solution(mesh):
    placed = (P("win", "pair", None, None), P(), P(), P("pair"))
    return jax.shard_map(
        local, mesh=mesh, in_specs=placed, out_specs=P("pair", "win"), check_vma=False
    )
```

```python
import functools
import math

import jax
import jax.numpy as jnp
from jax import lax
from jax.experimental import pallas as pl
from jax.experimental.pallas import tpu as pltpu
from jax.sharding import PartitionSpec as P

HALF = 3
BF = jnp.bfloat16
F32 = jnp.float32
VM = pl.BlockSpec(memory_space=pltpu.VMEM)
SM = pl.BlockSpec(memory_space=pltpu.SMEM)
ANY = pl.BlockSpec(memory_space=pl.ANY)

LANES = 128
SUBS = 16
LOW = 2 * SUBS
FAR_ROWS = 40
GROUP = 8


def moved(value, where):
    count = lax.axis_size("pair")
    pairs = [(i, where(i)) for i in range(count)]
    return lax.ppermute(value, "pair", [(a, b) for a, b in pairs if 0 <= b < count])


def swap(value):
    count = lax.axis_size("pair")
    return lax.ppermute(value, "pair", [(i, i ^ 1) for i in range(count)])


def whiten_into(ref, out_refs, first=0):
    windows, channels, rows, _ = ref.shape
    size = GROUP * rows
    r = lax.broadcasted_iota(jnp.int32, (size, size), 0)
    c = lax.broadcasted_iota(jnp.int32, (size, size), 1)
    source = (r // rows) * rows + 2 * (r % SUBS) + (r // SUBS) % 2
    perm = jnp.where(c == source, 1.0, 0.0).astype(BF)

    for v in range(windows):
        for g in range(channels // GROUP):
            values = ref[v, pl.ds(g * GROUP, GROUP)].astype(F32)
            power = jnp.sum(jnp.sum(values * values, axis=1), axis=1, keepdims=True)
            power = power * (1.0 / (rows * LANES))
            scaled = (values * lax.rsqrt(power + 1e-06)[:, :, None]).astype(BF)
            ordered = jnp.dot(perm, scaled.reshape(size, LANES), preferred_element_type=F32)
            at = pl.ds(first + g * GROUP, GROUP)
            out_refs[v][at] = ordered.astype(BF).reshape(GROUP, rows, LANES)


def windows_of(ref):
    return [ref.at[v] for v in range(ref.shape[0])]


def own_kernel(own_ref, _, again_ref, out_ref):
    again_ref[...] = own_ref[...]
    whiten_into(own_ref, windows_of(out_ref))


def gather_kernel(own_ref, sib_ref, *refs):
    windows = own_ref.shape[0]
    *in_refs, raw_ref, _, near_ref = refs[:-windows]
    out_refs = refs[-windows:]
    whiten_into(raw_ref, out_refs)
    for v in range(windows):
        at = 0
        for ref in (own_ref.at[v], sib_ref.at[v], *in_refs[v::windows], out_refs[v]):
            near_ref[v, pl.ds(at, ref.shape[0])] = ref[...]
            at += ref.shape[0]


def forward_kernel(order_ref, raw_ref, _, *refs):
    *out_refs, head_ref, tail_ref = refs
    whiten_into(raw_ref, out_refs)
    head, tail = head_ref.shape[1], tail_ref.shape[1]
    for v, out_ref in enumerate(out_refs):
        for p in range(head):
            head_ref[v, p] = out_ref[order_ref[p]]
        for p in range(tail):
            tail_ref[v, p] = out_ref[order_ref[head + p]]


def late_kernel(*refs):
    *swapped_refs, head_ref, tail_ref, out_ref = refs
    for v in range(out_ref.shape[0]):
        at = 0
        for ref in (swapped_refs[v], head_ref.at[v], tail_ref.at[v]):
            out_ref[v, pl.ds(at, ref.shape[0])] = ref[...]
            at += ref.shape[0]


def corr_kernel(
    first_ref,
    second_ref,
    live_ref,
    z_ref,
    near_ref,
    late_ref,
    weight_ref,
    fold_ref,
    wave_ref,
    keep_ref,
    up_ref,
    down_ref,
    cross,
    mid,
    corr,
):
    windows, early = near_ref.shape[:2]
    slots = mid.shape[1] // windows
    weight = weight_ref[...]
    alive = lax.broadcasted_iota(jnp.int32, (1, slots), 1) < live_ref[0]
    _, half_rows, wide, _ = up_ref.shape
    count = LANES // wide

    for v in range(windows):
        for g in range(slots // (2 * GROUP)):
            buf = g % 2
            for half in range(2):
                for q in range(GROUP):
                    p = g * 2 * GROUP + half * GROUP + q
                    a = near_ref[v, first_ref[p]].astype(F32)
                    at = second_ref[p]
                    b = jnp.where(
                        at < early,
                        near_ref[v, jnp.minimum(at, early - 1)],
                        late_ref[v, jnp.maximum(at - early, 0)],
                    ).astype(F32)
                    ar, ai, br, bi = a[:SUBS], a[SUBS:], b[:SUBS], b[SUBS:]
                    re = (ar * br + ai * bi) * weight
                    im = (ai * br - ar * bi) * weight
                    cols = pl.ds(half * LANES, LANES)
                    cross[buf, pl.ds(q * 2 * SUBS, SUBS), cols] = re.astype(BF)
                    cross[buf, pl.ds(q * 2 * SUBS + SUBS, SUBS), cols] = im.astype(BF)
            y = jnp.dot(fold_ref[...], cross[buf], preferred_element_type=F32)
            for part in range(2):
                z = y[part * LOW * GROUP : (part + 1) * LOW * GROUP]
                z = jnp.concatenate(
                    [
                        z[:, :LANES].reshape(LOW, GROUP, LANES),
                        z[:, LANES:].reshape(LOW, GROUP, LANES),
                    ],
                    axis=1,
                )
                rows = pl.ds(v * slots + g * 2 * GROUP, 2 * GROUP)
                mid[:, rows, pl.ds(part * LANES, LANES)] = z.astype(BF)

    def lags(t2, top):
        c = lax.dot_general(
            wave_ref[t2], mid[t2], (((1,), (1,)), ((), ())), preferred_element_type=F32
        )
        corr[t2] = c
        return jnp.maximum(top, jnp.abs(c))

    top = jnp.zeros((LANES, windows * slots), F32)
    top = lax.fori_loop(0, LOW, lags, top, unroll=True)
    peak = jnp.max(top, axis=0, keepdims=True) + 1e-06
    scale = [
        jnp.where(alive, 0.25 / peak[:, v * slots : (v + 1) * slots], 0.0)
        for v in range(windows)
    ]

    jobs = []
    for step, give_ref in ((1, up_ref), (-1, down_ref)):
        jobs += [(step, n, give_ref, n) for n in range(2)]
        jobs += [(-2 * step, n, give_ref, 2 + n) for n in range(2)]
        jobs += [(4, (1 + step) // 2, give_ref, 4)]
    for k, step in enumerate((0, -3, 3)):
        jobs += [(step, n, keep_ref, 2 * k + n) for n in range(2)]
    for step, n, ref, at in jobs:
        rows = pl.ds(lax.rem(z_ref[0] + step + count, count) * wide, wide)

        def emit(t, _, n=n, ref=ref, at=at, rows=rows):
            t2 = t + n * half_rows
            value = corr[t2, rows, pl.ds(0, slots)] * scale[0]
            for v in range(1, windows):
                value = value + corr[t2, rows, pl.ds(v * slots, slots)] * scale[v]
            ref[at, t] = value.astype(ref.dtype)
            return 0

        lax.fori_loop(0, half_rows, emit, 0, unroll=True)


def merge_kernel(keep_ref, left_ref, right_ref, own_ref, behind_ref, ahead_ref):
    for n in range(2):
        own_ref[n] = keep_ref[n] + left_ref[n].astype(F32) + right_ref[n].astype(F32)
        behind = keep_ref[2 + n] + left_ref[2 + n].astype(F32)
        ahead = keep_ref[4 + n] + right_ref[2 + n].astype(F32)
        if n == 0:
            behind = behind + right_ref[4].astype(F32)
        else:
            ahead = ahead + left_ref[4].astype(F32)
        behind_ref[n] = behind.astype(BF)
        ahead_ref[n] = ahead.astype(BF)


def final_kernel(own_ref, *refs):
    *other_refs, out_ref, total = refs
    halves, half_rows, wide, _ = own_ref.shape
    low = halves * half_rows
    for t2 in range(low):
        n, t = divmod(t2, half_rows)
        rows = own_ref[n, t]
        for ref in other_refs:
            rows = rows + ref[n, t].astype(F32)
        total[pl.ds(t2 * wide, wide)] = rows
    group = LANES // low
    for g in range(wide // group):
        rows = [total[pl.ds(g * group + t, low, stride=wide)] for t in range(group)]
        out_ref[:, pl.ds(g * LANES, LANES)] = jnp.concatenate(rows, axis=0).T


def table_kernel(sib_ref, _, fold_ref, wave_ref, sib_out_ref):
    def turns(rows, cols, period):
        r = lax.broadcasted_iota(jnp.int32, (rows, cols), 0)
        c = lax.broadcasted_iota(jnp.int32, (rows, cols), 1)
        angle = lax.rem(r * c, period).astype(F32) * (2.0 * math.pi / period)
        return jnp.cos(angle), jnp.sin(angle)

    whiten_into(sib_ref, windows_of(sib_out_ref))

    cos, sin = turns(LOW, SUBS, LOW)
    base = jnp.concatenate(
        [jnp.concatenate([cos, -sin], axis=1), jnp.concatenate([sin, cos], axis=1)], axis=0
    ).astype(BF)
    rows, cols = fold_ref.shape
    spread_rows = lax.broadcasted_iota(jnp.int32, (rows, 2 * LOW), 0) // GROUP
    spread_rows = spread_rows == lax.broadcasted_iota(jnp.int32, (rows, 2 * LOW), 1)
    spread_cols = lax.rem(lax.broadcasted_iota(jnp.int32, (2 * SUBS, cols), 1), 2 * SUBS)
    spread_cols = spread_cols == lax.broadcasted_iota(jnp.int32, (2 * SUBS, cols), 0)
    fold = jnp.dot(spread_rows.astype(F32).astype(BF), base, preferred_element_type=F32)
    fold = jnp.dot(
        fold.astype(BF), spread_cols.astype(F32).astype(BF), preferred_element_type=F32
    )
    q_row = lax.rem(lax.broadcasted_iota(jnp.int32, (rows, cols), 0), GROUP)
    q_col = lax.broadcasted_iota(jnp.int32, (rows, cols), 1) // (2 * SUBS)
    fold_ref[...] = jnp.where(q_row == q_col, fold, 0.0).astype(BF)

    low_cos, low_sin = turns(LOW, LANES, LOW * LANES)
    high_cos, high_sin = turns(LANES, LANES, LANES)
    for t2 in range(LOW):
        c, s = low_cos[t2 : t2 + 1], low_sin[t2 : t2 + 1]
        wave_ref[t2, :, pl.ds(0, LANES)] = (c * high_cos - s * high_sin).astype(BF)
        wave_ref[t2, :, pl.ds(LANES, LANES)] = (-s * high_cos - c * high_sin).astype(BF)


def far_order(pair_ends, ch_dev):
    block = jnp.arange(pair_ends.shape[0], dtype=jnp.int32)[:, None]
    away = (pair_ends[:, :, 1] // ch_dev - block) * (1 - 2 * (block % 2))
    named = jnp.where(away == -HALF, pair_ends[:, :, 1] % ch_dev, -1)
    channel = jnp.arange(ch_dev, dtype=jnp.int32)
    need = jnp.any(named[:, :, None] == channel, axis=1)
    count = jnp.sum(need.astype(jnp.int32), axis=1, keepdims=True)
    before = (channel[None, :] < channel[:, None])[None]
    rank = jnp.sum((before & need[:, None, :]).astype(jnp.int32), axis=2)
    return jnp.where(need, rank, count + channel - rank), count


def local(spectra, passband, pair_ends, live_pairs):
    win_count = lax.axis_size("win")
    win_dev, ch_dev, _, bins = spectra.shape
    slots = pair_ends.shape[1]
    rows = 2 * SUBS
    wide = LANES // win_count
    half = LOW // 2
    x = spectra.reshape(win_dev, ch_dev, 2, SUBS, LANES).transpose(0, 1, 3, 2, 4)
    x = x.reshape(win_dev, ch_dev, rows, LANES)
    me = lax.axis_index("pair")
    odd = me % 2
    place, named = far_order(pair_ends, ch_dev)
    target = jnp.clip(me - 1 + 2 * odd, 0, pair_ends.shape[0] - 1)
    channel = jnp.arange(ch_dev, dtype=jnp.int32)
    order = lax.dynamic_index_in_dim(place, target, 0, keepdims=False)
    order = jnp.sum(jnp.where(order[None, :] == channel[:, None], channel[None, :], 0), axis=1)

    ahead = moved(x, lambda i: i - 2 if i % 2 == 0 else i + 2)
    sib = swap(x)
    again, own = pl.pallas_call(
        own_kernel,
        out_shape=[jax.ShapeDtypeStruct(x.shape, BF)] * 2,
        in_specs=[VM, SM],
        out_specs=[VM] * 2,
        compiler_params=pltpu.CompilerParams(vmem_limit_bytes=16 << 20),
        cost_estimate=pl.CostEstimate(
            flops=1 << 30, bytes_accessed=2 << 20, transcendentals=0
        ),
    )(x, order)
    fold, wave, sib = pl.pallas_call(
        table_kernel,
        out_shape=[
            jax.ShapeDtypeStruct((2 * LOW * GROUP, 2 * SUBS * GROUP), BF),
            jax.ShapeDtypeStruct((LOW, LANES, 2 * LANES), BF),
            jax.ShapeDtypeStruct(x.shape, BF),
        ],
        in_specs=[VM, ANY],
        out_specs=[VM] * 3,
        compiler_params=pltpu.CompilerParams(vmem_limit_bytes=16 << 20),
        cost_estimate=pl.CostEstimate(
            flops=1 << 30, bytes_accessed=2 << 20, transcendentals=0
        ),
    )(sib, own)
    back = moved(again, lambda i: i + 2 if i % 2 == 0 else i - 2)
    *ahead, head, tail = pl.pallas_call(
        forward_kernel,
        out_shape=[jax.ShapeDtypeStruct(x.shape[1:], BF)] * win_dev
        + [
            jax.ShapeDtypeStruct((win_dev, FAR_ROWS, rows, LANES), BF),
            jax.ShapeDtypeStruct((win_dev, ch_dev - FAR_ROWS, rows, LANES), BF),
        ],
        in_specs=[SM, VM, ANY],
        out_specs=[VM] * (win_dev + 2),
        compiler_params=pltpu.CompilerParams(vmem_limit_bytes=16 << 20),
        cost_estimate=pl.CostEstimate(flops=0, bytes_accessed=0, transcendentals=0),
    )(order, ahead, fold)

    def outward(value):
        return moved(value, lambda i: i - 1 if i % 2 == 0 else i + 1)

    head = outward(head)
    tail = lax.cond(jnp.max(named) > FAR_ROWS, outward, jnp.zeros_like, tail)
    near, *back = pl.pallas_call(
        gather_kernel,
        out_shape=[
            jax.ShapeDtypeStruct((win_dev, 5 * ch_dev, rows, LANES), BF),
        ]
        + [jax.ShapeDtypeStruct(x.shape[1:], BF)] * win_dev,
        in_specs=[VM] * (3 + 2 * win_dev) + [ANY],
        out_specs=[VM] * (1 + win_dev),
        compiler_params=pltpu.CompilerParams(vmem_limit_bytes=24 << 20),
        cost_estimate=pl.CostEstimate(flops=0, bytes_accessed=0, transcendentals=0),
    )(own, sib, *ahead, *[swap(a) for a in ahead], back, tail)
    late = pl.pallas_call(
        late_kernel,
        out_shape=jax.ShapeDtypeStruct((win_dev, 2 * ch_dev, rows, LANES), BF),
        in_specs=[VM] * (win_dev + 2),
        out_specs=VM,
        compiler_params=pltpu.CompilerParams(vmem_limit_bytes=16 << 20),
        cost_estimate=pl.CostEstimate(
            flops=20 << 30, bytes_accessed=0, transcendentals=0
        ),
    )(*[swap(b) for b in back], head, tail)

    ends = lax.dynamic_index_in_dim(pair_ends, me, 0, keepdims=False)
    first = ends[:, 0] % ch_dev
    away = (ends[:, 1] // ch_dev - me) * (1 - 2 * odd)
    row = ends[:, 1] % ch_dev
    mine = lax.dynamic_index_in_dim(place, me, 0, keepdims=False)
    mine = jnp.sum(jnp.where(row[:, None] == channel[None, :], mine[None, :], 0), axis=1)
    row = jnp.where(away == -HALF, mine, row)
    second = jnp.zeros_like(away)
    for n, d in enumerate((0, 1, 2, -1, -2, 3, -3)):
        second = jnp.where(away == d, n * ch_dev + row, second)

    factor = jnp.where(jnp.arange(bins) == 0, 1.0, 2.0).astype(F32)
    weight = (passband * factor).reshape(SUBS, LANES)

    z = lax.axis_index("win")
    give = jax.ShapeDtypeStruct((5, half, wide, slots), BF)
    keep, up, down = pl.pallas_call(
        corr_kernel,
        out_shape=[jax.ShapeDtypeStruct((6, half, wide, slots), F32), give, give],
        in_specs=[SM] * 4 + [VM] * 5,
        out_specs=[VM] * 3,
        scratch_shapes=[
            pltpu.VMEM((2, GROUP * rows, 2 * LANES), BF),
            pltpu.VMEM((LOW, win_dev * slots, 2 * LANES), BF),
            pltpu.VMEM((LOW, LANES, win_dev * slots), F32),
        ],
        compiler_params=pltpu.CompilerParams(vmem_limit_bytes=32 << 20),
        cost_estimate=pl.CostEstimate(
            flops=8 << 30, bytes_accessed=8 << 20, transcendentals=0
        ),
    )(first, second, live_pairs, z.reshape(1), near, late, weight, fold, wave)

    def along(value, step):
        return lax.ppermute(
            value, "win", [(i, (i + step) % win_count) for i in range(win_count)]
        )

    piece = (2, half, wide, slots)
    mine, behind, ahead = pl.pallas_call(
        merge_kernel,
        out_shape=[jax.ShapeDtypeStruct(piece, d) for d in (F32, BF, BF)],
        in_specs=[VM] * 3,
        out_specs=[VM] * 3,
        compiler_params=pltpu.CompilerParams(vmem_limit_bytes=16 << 20),
    )(keep, along(up, 1), along(down, -1))
    return pl.pallas_call(
        final_kernel,
        out_shape=jax.ShapeDtypeStruct((slots, LOW * wide), F32),
        in_specs=[VM] * 3,
        out_specs=VM,
        scratch_shapes=[pltpu.VMEM((LOW * wide, slots), F32)],
    )(mine, along(behind, -3), along(ahead, 3))


def solution(mesh):
    placed = (P("win", "pair", None, None), P(), P(), P("pair"))
    return jax.shard_map(
        local, mesh=mesh, in_specs=placed, out_specs=P("pair", "win"), check_vma=False
    )
```

```python
import functools
import math

import jax
import jax.numpy as jnp
from jax import lax
from jax.experimental import pallas as pl
from jax.experimental.pallas import tpu as pltpu
from jax.sharding import PartitionSpec as P

HALF = 3
BF = jnp.bfloat16
F32 = jnp.float32
VM = pl.BlockSpec(memory_space=pltpu.VMEM)
SM = pl.BlockSpec(memory_space=pltpu.SMEM)
ANY = pl.BlockSpec(memory_space=pl.ANY)

LANES = 128
SUBS = 16
LOW = 2 * SUBS
FAR_ROWS = 40
GROUP = 8


def moved(value, where):
    count = lax.axis_size("pair")
    pairs = [(i, where(i)) for i in range(count)]
    return lax.ppermute(value, "pair", [(a, b) for a, b in pairs if 0 <= b < count])


def swap(value):
    count = lax.axis_size("pair")
    return lax.ppermute(value, "pair", [(i, i ^ 1) for i in range(count)])


def whiten_into(ref, out_refs, first=0):
    windows, channels, rows, _ = ref.shape
    size = GROUP * rows
    r = lax.broadcasted_iota(jnp.int32, (size, size), 0)
    c = lax.broadcasted_iota(jnp.int32, (size, size), 1)
    source = (r // rows) * rows + 2 * (r % SUBS) + (r // SUBS) % 2
    perm = jnp.where(c == source, 1.0, 0.0).astype(BF)

    for v in range(windows):
        for g in range(channels // GROUP):
            values = ref[v, pl.ds(g * GROUP, GROUP)].astype(F32)
            power = jnp.sum(jnp.sum(values * values, axis=1), axis=1, keepdims=True)
            power = power * (1.0 / (rows * LANES))
            scaled = (values * lax.rsqrt(power + 1e-06)[:, :, None]).astype(BF)
            ordered = jnp.dot(perm, scaled.reshape(size, LANES), preferred_element_type=F32)
            at = pl.ds(first + g * GROUP, GROUP)
            out_refs[v][at] = ordered.astype(BF).reshape(GROUP, rows, LANES)


def windows_of(ref):
    return [ref.at[v] for v in range(ref.shape[0])]


def own_kernel(own_ref, _, again_ref, out_ref):
    again_ref[...] = own_ref[...]
    whiten_into(own_ref, windows_of(out_ref))


def gather_kernel(own_ref, sib_ref, *refs):
    windows = own_ref.shape[0]
    *in_refs, raw_ref, _, near_ref = refs[:-windows]
    out_refs = refs[-windows:]
    whiten_into(raw_ref, out_refs)
    for v in range(windows):
        at = 0
        for ref in (own_ref.at[v], sib_ref.at[v], *in_refs[v::windows], out_refs[v]):
            near_ref[v, pl.ds(at, ref.shape[0])] = ref[...]
            at += ref.shape[0]


def forward_kernel(order_ref, raw_ref, _, *refs):
    *out_refs, head_ref, tail_ref = refs
    whiten_into(raw_ref, out_refs)
    head, tail = head_ref.shape[1], tail_ref.shape[1]
    for v, out_ref in enumerate(out_refs):
        for p in range(head):
            head_ref[v, p] = out_ref[order_ref[p]]
        for p in range(tail):
            tail_ref[v, p] = out_ref[order_ref[head + p]]


def late_kernel(*refs):
    *swapped_refs, head_ref, tail_ref, out_ref = refs
    for v in range(out_ref.shape[0]):
        at = 0
        for ref in (swapped_refs[v], head_ref.at[v], tail_ref.at[v]):
            out_ref[v, pl.ds(at, ref.shape[0])] = ref[...]
            at += ref.shape[0]


def corr_kernel(
    first_ref,
    second_ref,
    live_ref,
    z_ref,
    near_ref,
    late_ref,
    weight_ref,
    fold_ref,
    wave_ref,
    keep_ref,
    up_ref,
    down_ref,
    cross,
    mid,
    corr,
):
    windows, early = near_ref.shape[:2]
    slots = mid.shape[1] // windows
    weight = weight_ref[...]
    alive = lax.broadcasted_iota(jnp.int32, (1, slots), 1) < live_ref[0]
    _, half_rows, wide, _ = up_ref.shape
    count = LANES // wide

    for v in range(windows):
        for g in range(slots // (2 * GROUP)):
            buf = g % 2
            for half in range(2):
                for q in range(GROUP):
                    p = g * 2 * GROUP + half * GROUP + q
                    a = near_ref[v, first_ref[p]].astype(F32)
                    at = second_ref[p]
                    b = jnp.where(
                        at < early,
                        near_ref[v, jnp.minimum(at, early - 1)],
                        late_ref[v, jnp.maximum(at - early, 0)],
                    ).astype(F32)
                    ar, ai, br, bi = a[:SUBS], a[SUBS:], b[:SUBS], b[SUBS:]
                    re = (ar * br + ai * bi) * weight
                    im = (ai * br - ar * bi) * weight
                    cols = pl.ds(half * LANES, LANES)
                    cross[buf, pl.ds(q * 2 * SUBS, SUBS), cols] = re.astype(BF)
                    cross[buf, pl.ds(q * 2 * SUBS + SUBS, SUBS), cols] = im.astype(BF)
            y = jnp.dot(fold_ref[...], cross[buf], preferred_element_type=F32)
            for part in range(2):
                z = y[part * LOW * GROUP : (part + 1) * LOW * GROUP]
                z = jnp.concatenate(
                    [
                        z[:, :LANES].reshape(LOW, GROUP, LANES),
                        z[:, LANES:].reshape(LOW, GROUP, LANES),
                    ],
                    axis=1,
                )
                rows = pl.ds(v * slots + g * 2 * GROUP, 2 * GROUP)
                mid[:, rows, pl.ds(part * LANES, LANES)] = z.astype(BF)

    def lags(t2, top):
        c = lax.dot_general(
            wave_ref[t2], mid[t2], (((1,), (1,)), ((), ())), preferred_element_type=F32
        )
        corr[t2] = c
        return jnp.maximum(top, jnp.abs(c))

    top = jnp.zeros((LANES, windows * slots), F32)
    top = lax.fori_loop(0, LOW, lags, top, unroll=True)
    peak = jnp.max(top, axis=0, keepdims=True) + 1e-06
    scale = [
        jnp.where(alive, 0.25 / peak[:, v * slots : (v + 1) * slots], 0.0)
        for v in range(windows)
    ]

    jobs = []
    for step, give_ref in ((1, up_ref), (-1, down_ref)):
        jobs += [(step, n, give_ref, n) for n in range(2)]
        jobs += [(-2 * step, n, give_ref, 2 + n) for n in range(2)]
        jobs += [(4, (1 + step) // 2, give_ref, 4)]
    for k, step in enumerate((0, -3, 3)):
        jobs += [(step, n, keep_ref, 2 * k + n) for n in range(2)]
    for step, n, ref, at in jobs:
        rows = pl.ds(lax.rem(z_ref[0] + step + count, count) * wide, wide)

        def emit(t, _, n=n, ref=ref, at=at, rows=rows):
            t2 = t + n * half_rows
            value = corr[t2, rows, pl.ds(0, slots)] * scale[0]
            for v in range(1, windows):
                value = value + corr[t2, rows, pl.ds(v * slots, slots)] * scale[v]
            ref[at, t] = value.astype(ref.dtype)
            return 0

        lax.fori_loop(0, half_rows, emit, 0, unroll=True)


def merge_kernel(keep_ref, left_ref, right_ref, own_ref, behind_ref, ahead_ref):
    for n in range(2):
        own_ref[n] = keep_ref[n] + left_ref[n].astype(F32) + right_ref[n].astype(F32)
        behind = keep_ref[2 + n] + left_ref[2 + n].astype(F32)
        ahead = keep_ref[4 + n] + right_ref[2 + n].astype(F32)
        if n == 0:
            behind = behind + right_ref[4].astype(F32)
        else:
            ahead = ahead + left_ref[4].astype(F32)
        behind_ref[n] = behind.astype(BF)
        ahead_ref[n] = ahead.astype(BF)


def final_kernel(own_ref, *refs):
    *other_refs, out_ref, total = refs
    halves, half_rows, wide, _ = own_ref.shape
    low = halves * half_rows
    for t2 in range(low):
        n, t = divmod(t2, half_rows)
        rows = own_ref[n, t]
        for ref in other_refs:
            rows = rows + ref[n, t].astype(F32)
        total[pl.ds(t2 * wide, wide)] = rows
    group = LANES // low
    for g in range(wide // group):
        rows = [total[pl.ds(g * group + t, low, stride=wide)] for t in range(group)]
        out_ref[:, pl.ds(g * LANES, LANES)] = jnp.concatenate(rows, axis=0).T


def table_kernel(sib_ref, _, fold_ref, wave_ref, sib_out_ref):
    def turns(rows, cols, period):
        r = lax.broadcasted_iota(jnp.int32, (rows, cols), 0)
        c = lax.broadcasted_iota(jnp.int32, (rows, cols), 1)
        angle = lax.rem(r * c, period).astype(F32) * (2.0 * math.pi / period)
        return jnp.cos(angle), jnp.sin(angle)

    whiten_into(sib_ref, windows_of(sib_out_ref))

    cos, sin = turns(LOW, SUBS, LOW)
    base = jnp.concatenate(
        [jnp.concatenate([cos, -sin], axis=1), jnp.concatenate([sin, cos], axis=1)], axis=0
    ).astype(BF)
    rows, cols = fold_ref.shape
    spread_rows = lax.broadcasted_iota(jnp.int32, (rows, 2 * LOW), 0) // GROUP
    spread_rows = spread_rows == lax.broadcasted_iota(jnp.int32, (rows, 2 * LOW), 1)
    spread_cols = lax.rem(lax.broadcasted_iota(jnp.int32, (2 * SUBS, cols), 1), 2 * SUBS)
    spread_cols = spread_cols == lax.broadcasted_iota(jnp.int32, (2 * SUBS, cols), 0)
    fold = jnp.dot(spread_rows.astype(F32).astype(BF), base, preferred_element_type=F32)
    fold = jnp.dot(
        fold.astype(BF), spread_cols.astype(F32).astype(BF), preferred_element_type=F32
    )
    q_row = lax.rem(lax.broadcasted_iota(jnp.int32, (rows, cols), 0), GROUP)
    q_col = lax.broadcasted_iota(jnp.int32, (rows, cols), 1) // (2 * SUBS)
    fold_ref[...] = jnp.where(q_row == q_col, fold, 0.0).astype(BF)

    low_cos, low_sin = turns(LOW, LANES, LOW * LANES)
    high_cos, high_sin = turns(LANES, LANES, LANES)
    for t2 in range(LOW):
        c, s = low_cos[t2 : t2 + 1], low_sin[t2 : t2 + 1]
        wave_ref[t2, :, pl.ds(0, LANES)] = (c * high_cos - s * high_sin).astype(BF)
        wave_ref[t2, :, pl.ds(LANES, LANES)] = (-s * high_cos - c * high_sin).astype(BF)


def far_order(pair_ends, ch_dev):
    block = jnp.arange(pair_ends.shape[0], dtype=jnp.int32)[:, None]
    away = (pair_ends[:, :, 1] // ch_dev - block) * (1 - 2 * (block % 2))
    named = jnp.where(away == -HALF, pair_ends[:, :, 1] % ch_dev, -1)
    channel = jnp.arange(ch_dev, dtype=jnp.int32)
    need = jnp.any(named[:, :, None] == channel, axis=1)
    count = jnp.sum(need.astype(jnp.int32), axis=1, keepdims=True)
    before = (channel[None, :] < channel[:, None])[None]
    rank = jnp.sum((before & need[:, None, :]).astype(jnp.int32), axis=2)
    return jnp.where(need, rank, count + channel - rank), count


def local(spectra, passband, pair_ends, live_pairs):
    win_count = lax.axis_size("win")
    win_dev, ch_dev, _, bins = spectra.shape
    slots = pair_ends.shape[1]
    rows = 2 * SUBS
    wide = LANES // win_count
    half = LOW // 2
    x = spectra.reshape(win_dev, ch_dev, 2, SUBS, LANES).transpose(0, 1, 3, 2, 4)
    x = x.reshape(win_dev, ch_dev, rows, LANES)
    me = lax.axis_index("pair")
    odd = me % 2
    place, named = far_order(pair_ends, ch_dev)
    target = jnp.clip(me - 1 + 2 * odd, 0, pair_ends.shape[0] - 1)
    channel = jnp.arange(ch_dev, dtype=jnp.int32)
    order = lax.dynamic_index_in_dim(place, target, 0, keepdims=False)
    order = jnp.sum(jnp.where(order[None, :] == channel[:, None], channel[None, :], 0), axis=1)

    ahead = moved(x, lambda i: i - 2 if i % 2 == 0 else i + 2)
    sib = swap(x)
    again, own = pl.pallas_call(
        own_kernel,
        out_shape=[jax.ShapeDtypeStruct(x.shape, BF)] * 2,
        in_specs=[VM, SM],
        out_specs=[VM] * 2,
        compiler_params=pltpu.CompilerParams(vmem_limit_bytes=16 << 20),
        cost_estimate=pl.CostEstimate(
            flops=1 << 30, bytes_accessed=2 << 20, transcendentals=0
        ),
    )(x, order)
    fold, wave, sib = pl.pallas_call(
        table_kernel,
        out_shape=[
            jax.ShapeDtypeStruct((2 * LOW * GROUP, 2 * SUBS * GROUP), BF),
            jax.ShapeDtypeStruct((LOW, LANES, 2 * LANES), BF),
            jax.ShapeDtypeStruct(x.shape, BF),
        ],
        in_specs=[VM, ANY],
        out_specs=[VM] * 3,
        compiler_params=pltpu.CompilerParams(vmem_limit_bytes=16 << 20),
        cost_estimate=pl.CostEstimate(
            flops=1 << 30, bytes_accessed=2 << 20, transcendentals=0
        ),
    )(sib, own)
    back = moved(again, lambda i: i + 2 if i % 2 == 0 else i - 2)
    *ahead, head, tail = pl.pallas_call(
        forward_kernel,
        out_shape=[jax.ShapeDtypeStruct(x.shape[1:], BF)] * win_dev
        + [
            jax.ShapeDtypeStruct((win_dev, FAR_ROWS, rows, LANES), BF),
            jax.ShapeDtypeStruct((win_dev, ch_dev - FAR_ROWS, rows, LANES), BF),
        ],
        in_specs=[SM, VM, ANY],
        out_specs=[VM] * (win_dev + 2),
        compiler_params=pltpu.CompilerParams(vmem_limit_bytes=16 << 20),
        cost_estimate=pl.CostEstimate(flops=0, bytes_accessed=0, transcendentals=0),
    )(order, ahead, fold)

    def outward(value):
        return moved(value, lambda i: i - 1 if i % 2 == 0 else i + 1)

    head = outward(head)
    tail = lax.cond(jnp.max(named) > FAR_ROWS, outward, jnp.zeros_like, tail)
    near, *back = pl.pallas_call(
        gather_kernel,
        out_shape=[
            jax.ShapeDtypeStruct((win_dev, 5 * ch_dev, rows, LANES), BF),
        ]
        + [jax.ShapeDtypeStruct(x.shape[1:], BF)] * win_dev,
        in_specs=[VM] * (3 + 2 * win_dev) + [ANY],
        out_specs=[VM] * (1 + win_dev),
        compiler_params=pltpu.CompilerParams(vmem_limit_bytes=24 << 20),
        cost_estimate=pl.CostEstimate(flops=0, bytes_accessed=0, transcendentals=0),
    )(own, sib, *ahead, *[swap(a) for a in ahead], back, tail)
    late = pl.pallas_call(
        late_kernel,
        out_shape=jax.ShapeDtypeStruct((win_dev, 2 * ch_dev, rows, LANES), BF),
        in_specs=[VM] * (win_dev + 2),
        out_specs=VM,
        compiler_params=pltpu.CompilerParams(vmem_limit_bytes=16 << 20),
        cost_estimate=pl.CostEstimate(
            flops=20 << 30, bytes_accessed=0, transcendentals=0
        ),
    )(*[swap(b) for b in back], head, tail)

    ends = lax.dynamic_index_in_dim(pair_ends, me, 0, keepdims=False)
    first = ends[:, 0] % ch_dev
    away = (ends[:, 1] // ch_dev - me) * (1 - 2 * odd)
    row = ends[:, 1] % ch_dev
    mine = lax.dynamic_index_in_dim(place, me, 0, keepdims=False)
    mine = jnp.sum(jnp.where(row[:, None] == channel[None, :], mine[None, :], 0), axis=1)
    row = jnp.where(away == -HALF, mine, row)
    second = jnp.zeros_like(away)
    for n, d in enumerate((0, 1, 2, -1, -2, 3, -3)):
        second = jnp.where(away == d, n * ch_dev + row, second)

    factor = jnp.where(jnp.arange(bins) == 0, 1.0, 2.0).astype(F32)
    weight = (passband * factor).reshape(SUBS, LANES)

    z = lax.axis_index("win")
    give = jax.ShapeDtypeStruct((5, half, wide, slots), BF)
    keep, up, down = pl.pallas_call(
        corr_kernel,
        out_shape=[jax.ShapeDtypeStruct((6, half, wide, slots), F32), give, give],
        in_specs=[SM] * 4 + [VM] * 5,
        out_specs=[VM] * 3,
        scratch_shapes=[
            pltpu.VMEM((2, GROUP * rows, 2 * LANES), BF),
            pltpu.VMEM((LOW, win_dev * slots, 2 * LANES), BF),
            pltpu.VMEM((LOW, LANES, win_dev * slots), F32),
        ],
        compiler_params=pltpu.CompilerParams(vmem_limit_bytes=32 << 20),
        cost_estimate=pl.CostEstimate(
            flops=8 << 30, bytes_accessed=8 << 20, transcendentals=0
        ),
    )(first, second, live_pairs, z.reshape(1), near, late, weight, fold, wave)

    def along(value, step):
        return lax.ppermute(
            value, "win", [(i, (i + step) % win_count) for i in range(win_count)]
        )

    piece = (2, half, wide, slots)
    mine, behind, ahead = pl.pallas_call(
        merge_kernel,
        out_shape=[jax.ShapeDtypeStruct(piece, d) for d in (F32, BF, BF)],
        in_specs=[VM] * 3,
        out_specs=[VM] * 3,
        compiler_params=pltpu.CompilerParams(vmem_limit_bytes=8 << 20),
    )(keep, along(up, 1), along(down, -1))
    return pl.pallas_call(
        final_kernel,
        out_shape=jax.ShapeDtypeStruct((slots, LOW * wide), F32),
        in_specs=[VM] * 3,
        out_specs=VM,
        scratch_shapes=[pltpu.VMEM((LOW * wide, slots), F32)],
        compiler_params=pltpu.CompilerParams(vmem_limit_bytes=8 << 20),
    )(mine, along(behind, -3), along(ahead, 3))


def solution(mesh):
    placed = (P("win", "pair", None, None), P(), P(), P("pair"))
    return jax.shard_map(
        local, mesh=mesh, in_specs=placed, out_specs=P("pair", "win"), check_vma=False
    )
```

```python
import functools
import math

import jax
import jax.numpy as jnp
from jax import lax
from jax.experimental import pallas as pl
from jax.experimental.pallas import tpu as pltpu
from jax.sharding import PartitionSpec as P

HALF = 3
BF = jnp.bfloat16
F32 = jnp.float32
VM = pl.BlockSpec(memory_space=pltpu.VMEM)
SM = pl.BlockSpec(memory_space=pltpu.SMEM)
ANY = pl.BlockSpec(memory_space=pl.ANY)

LANES = 128
SUBS = 16
LOW = 2 * SUBS
FAR_ROWS = 40
GROUP = 8


def moved(value, where):
    count = lax.axis_size("pair")
    pairs = [(i, where(i)) for i in range(count)]
    return lax.ppermute(value, "pair", [(a, b) for a, b in pairs if 0 <= b < count])


def swap(value):
    count = lax.axis_size("pair")
    return lax.ppermute(value, "pair", [(i, i ^ 1) for i in range(count)])


def whiten_into(ref, out_refs, first=0):
    windows, channels, rows, _ = ref.shape
    size = GROUP * rows
    r = lax.broadcasted_iota(jnp.int32, (size, size), 0)
    c = lax.broadcasted_iota(jnp.int32, (size, size), 1)
    source = (r // rows) * rows + 2 * (r % SUBS) + (r // SUBS) % 2
    perm = jnp.where(c == source, 1.0, 0.0).astype(BF)

    for v in range(windows):
        for g in range(channels // GROUP):
            values = ref[v, pl.ds(g * GROUP, GROUP)].astype(F32)
            power = jnp.sum(jnp.sum(values * values, axis=1), axis=1, keepdims=True)
            power = power * (1.0 / (rows * LANES))
            scaled = (values * lax.rsqrt(power + 1e-06)[:, :, None]).astype(BF)
            ordered = jnp.dot(perm, scaled.reshape(size, LANES), preferred_element_type=F32)
            at = pl.ds(first + g * GROUP, GROUP)
            out_refs[v][at] = ordered.astype(BF).reshape(GROUP, rows, LANES)


def windows_of(ref):
    return [ref.at[v] for v in range(ref.shape[0])]


def own_kernel(own_ref, _, again_ref, out_ref):
    again_ref[...] = own_ref[...]
    whiten_into(own_ref, windows_of(out_ref))


def lay(refs, out_ref, sem):
    copies = []
    at = 0
    for n, ref in enumerate(refs):
        copies.append(pltpu.make_async_copy(ref, out_ref.at[pl.ds(at, ref.shape[0])], sem.at[n]))
        copies[-1].start()
        at += ref.shape[0]
    return copies, at


def gather_kernel(own_ref, sib_ref, *refs):
    windows = own_ref.shape[0]
    *in_refs, raw_ref, _, near_ref = refs[: -windows - 1]
    out_refs, sem = refs[-windows - 1 : -1], refs[-1]
    copies = []
    for v in range(windows):
        parts = (own_ref.at[v], sib_ref.at[v], *in_refs[v::windows])
        more, at = lay(parts, near_ref.at[v], sem.at[v])
        copies += more
    whiten_into(raw_ref, out_refs)
    for v in range(windows):
        near_ref[v, pl.ds(at, raw_ref.shape[1])] = out_refs[v][...]
    for copy in copies:
        copy.wait()


def forward_kernel(order_ref, raw_ref, _, *refs):
    *out_refs, head_ref, tail_ref = refs
    whiten_into(raw_ref, out_refs)
    head, tail = head_ref.shape[1], tail_ref.shape[1]
    for v, out_ref in enumerate(out_refs):
        for p in range(head):
            head_ref[v, p] = out_ref[order_ref[p]]
        for p in range(tail):
            tail_ref[v, p] = out_ref[order_ref[head + p]]


def late_kernel(*refs):
    *swapped_refs, head_ref, tail_ref, out_ref, sem = refs
    copies = []
    for v in range(out_ref.shape[0]):
        parts = (swapped_refs[v], head_ref.at[v], tail_ref.at[v])
        copies += lay(parts, out_ref.at[v], sem.at[v])[0]
    for copy in copies:
        copy.wait()


def corr_kernel(
    first_ref,
    second_ref,
    live_ref,
    z_ref,
    near_ref,
    late_ref,
    weight_ref,
    fold_ref,
    wave_ref,
    keep_ref,
    up_ref,
    down_ref,
    cross,
    mid,
    corr,
):
    windows, early = near_ref.shape[:2]
    slots = mid.shape[1] // windows
    weight = weight_ref[...]
    alive = lax.broadcasted_iota(jnp.int32, (1, slots), 1) < live_ref[0]
    _, half_rows, wide, _ = up_ref.shape
    count = LANES // wide

    for v in range(windows):
        for g in range(slots // (2 * GROUP)):
            buf = g % 2
            for half in range(2):
                for q in range(GROUP):
                    p = g * 2 * GROUP + half * GROUP + q
                    a = near_ref[v, first_ref[p]].astype(F32)
                    at = second_ref[p]
                    b = jnp.where(
                        at < early,
                        near_ref[v, jnp.minimum(at, early - 1)],
                        late_ref[v, jnp.maximum(at - early, 0)],
                    ).astype(F32)
                    ar, ai, br, bi = a[:SUBS], a[SUBS:], b[:SUBS], b[SUBS:]
                    re = (ar * br + ai * bi) * weight
                    im = (ai * br - ar * bi) * weight
                    cols = pl.ds(half * LANES, LANES)
                    cross[buf, pl.ds(q * 2 * SUBS, SUBS), cols] = re.astype(BF)
                    cross[buf, pl.ds(q * 2 * SUBS + SUBS, SUBS), cols] = im.astype(BF)
            y = jnp.dot(fold_ref[...], cross[buf], preferred_element_type=F32)
            for part in range(2):
                z = y[part * LOW * GROUP : (part + 1) * LOW * GROUP]
                z = jnp.concatenate(
                    [
                        z[:, :LANES].reshape(LOW, GROUP, LANES),
                        z[:, LANES:].reshape(LOW, GROUP, LANES),
                    ],
                    axis=1,
                )
                rows = pl.ds(v * slots + g * 2 * GROUP, 2 * GROUP)
                mid[:, rows, pl.ds(part * LANES, LANES)] = z.astype(BF)

    def lags(t2, top):
        c = lax.dot_general(
            wave_ref[t2], mid[t2], (((1,), (1,)), ((), ())), preferred_element_type=F32
        )
        corr[t2] = c
        return jnp.maximum(top, jnp.abs(c))

    top = jnp.zeros((LANES, windows * slots), F32)
    top = lax.fori_loop(0, LOW, lags, top, unroll=True)
    peak = jnp.max(top, axis=0, keepdims=True) + 1e-06
    scale = [
        jnp.where(alive, 0.25 / peak[:, v * slots : (v + 1) * slots], 0.0)
        for v in range(windows)
    ]

    jobs = []
    for step, give_ref in ((1, up_ref), (-1, down_ref)):
        jobs += [(step, n, give_ref, n) for n in range(2)]
        jobs += [(-2 * step, n, give_ref, 2 + n) for n in range(2)]
        jobs += [(4, (1 + step) // 2, give_ref, 4)]
    for k, step in enumerate((0, -3, 3)):
        jobs += [(step, n, keep_ref, 2 * k + n) for n in range(2)]
    for step, n, ref, at in jobs:
        rows = pl.ds(lax.rem(z_ref[0] + step + count, count) * wide, wide)

        def emit(t, _, n=n, ref=ref, at=at, rows=rows):
            t2 = t + n * half_rows
            value = corr[t2, rows, pl.ds(0, slots)] * scale[0]
            for v in range(1, windows):
                value = value + corr[t2, rows, pl.ds(v * slots, slots)] * scale[v]
            ref[at, t] = value.astype(ref.dtype)
            return 0

        lax.fori_loop(0, half_rows, emit, 0, unroll=True)


def merge_kernel(keep_ref, left_ref, right_ref, own_ref, behind_ref, ahead_ref):
    for n in range(2):
        own_ref[n] = keep_ref[n] + left_ref[n].astype(F32) + right_ref[n].astype(F32)
        behind = keep_ref[2 + n] + left_ref[2 + n].astype(F32)
        ahead = keep_ref[4 + n] + right_ref[2 + n].astype(F32)
        if n == 0:
            behind = behind + right_ref[4].astype(F32)
        else:
            ahead = ahead + left_ref[4].astype(F32)
        behind_ref[n] = behind.astype(BF)
        ahead_ref[n] = ahead.astype(BF)


def final_kernel(own_ref, *refs):
    *other_refs, out_ref, total = refs
    halves, half_rows, wide, _ = own_ref.shape
    low = halves * half_rows
    for t2 in range(low):
        n, t = divmod(t2, half_rows)
        rows = own_ref[n, t]
        for ref in other_refs:
            rows = rows + ref[n, t].astype(F32)
        total[pl.ds(t2 * wide, wide)] = rows
    group = LANES // low
    for g in range(wide // group):
        rows = [total[pl.ds(g * group + t, low, stride=wide)] for t in range(group)]
        out_ref[:, pl.ds(g * LANES, LANES)] = jnp.concatenate(rows, axis=0).T


def table_kernel(sib_ref, _, fold_ref, wave_ref, sib_out_ref):
    def turns(rows, cols, period):
        r = lax.broadcasted_iota(jnp.int32, (rows, cols), 0)
        c = lax.broadcasted_iota(jnp.int32, (rows, cols), 1)
        angle = lax.rem(r * c, period).astype(F32) * (2.0 * math.pi / period)
        return jnp.cos(angle), jnp.sin(angle)

    whiten_into(sib_ref, windows_of(sib_out_ref))

    cos, sin = turns(LOW, SUBS, LOW)
    base = jnp.concatenate(
        [jnp.concatenate([cos, -sin], axis=1), jnp.concatenate([sin, cos], axis=1)], axis=0
    ).astype(BF)
    rows, cols = fold_ref.shape
    spread_rows = lax.broadcasted_iota(jnp.int32, (rows, 2 * LOW), 0) // GROUP
    spread_rows = spread_rows == lax.broadcasted_iota(jnp.int32, (rows, 2 * LOW), 1)
    spread_cols = lax.rem(lax.broadcasted_iota(jnp.int32, (2 * SUBS, cols), 1), 2 * SUBS)
    spread_cols = spread_cols == lax.broadcasted_iota(jnp.int32, (2 * SUBS, cols), 0)
    fold = jnp.dot(spread_rows.astype(F32).astype(BF), base, preferred_element_type=F32)
    fold = jnp.dot(
        fold.astype(BF), spread_cols.astype(F32).astype(BF), preferred_element_type=F32
    )
    q_row = lax.rem(lax.broadcasted_iota(jnp.int32, (rows, cols), 0), GROUP)
    q_col = lax.broadcasted_iota(jnp.int32, (rows, cols), 1) // (2 * SUBS)
    fold_ref[...] = jnp.where(q_row == q_col, fold, 0.0).astype(BF)

    low_cos, low_sin = turns(LOW, LANES, LOW * LANES)
    high_cos, high_sin = turns(LANES, LANES, LANES)
    for t2 in range(LOW):
        c, s = low_cos[t2 : t2 + 1], low_sin[t2 : t2 + 1]
        wave_ref[t2, :, pl.ds(0, LANES)] = (c * high_cos - s * high_sin).astype(BF)
        wave_ref[t2, :, pl.ds(LANES, LANES)] = (-s * high_cos - c * high_sin).astype(BF)


def far_order(pair_ends, ch_dev):
    block = jnp.arange(pair_ends.shape[0], dtype=jnp.int32)[:, None]
    away = (pair_ends[:, :, 1] // ch_dev - block) * (1 - 2 * (block % 2))
    named = jnp.where(away == -HALF, pair_ends[:, :, 1] % ch_dev, -1)
    channel = jnp.arange(ch_dev, dtype=jnp.int32)
    need = jnp.any(named[:, :, None] == channel, axis=1)
    count = jnp.sum(need.astype(jnp.int32), axis=1, keepdims=True)
    before = (channel[None, :] < channel[:, None])[None]
    rank = jnp.sum((before & need[:, None, :]).astype(jnp.int32), axis=2)
    return jnp.where(need, rank, count + channel - rank), count


def local(spectra, passband, pair_ends, live_pairs):
    win_count = lax.axis_size("win")
    win_dev, ch_dev, _, bins = spectra.shape
    slots = pair_ends.shape[1]
    rows = 2 * SUBS
    wide = LANES // win_count
    half = LOW // 2
    x = spectra.reshape(win_dev, ch_dev, 2, SUBS, LANES).transpose(0, 1, 3, 2, 4)
    x = x.reshape(win_dev, ch_dev, rows, LANES)
    me = lax.axis_index("pair")
    odd = me % 2
    place, named = far_order(pair_ends, ch_dev)
    target = jnp.clip(me - 1 + 2 * odd, 0, pair_ends.shape[0] - 1)
    channel = jnp.arange(ch_dev, dtype=jnp.int32)
    order = lax.dynamic_index_in_dim(place, target, 0, keepdims=False)
    order = jnp.sum(jnp.where(order[None, :] == channel[:, None], channel[None, :], 0), axis=1)

    ahead = moved(x, lambda i: i - 2 if i % 2 == 0 else i + 2)
    sib = swap(x)
    again, own = pl.pallas_call(
        own_kernel,
        out_shape=[jax.ShapeDtypeStruct(x.shape, BF)] * 2,
        in_specs=[VM, SM],
        out_specs=[VM] * 2,
        compiler_params=pltpu.CompilerParams(vmem_limit_bytes=16 << 20),
        cost_estimate=pl.CostEstimate(
            flops=1 << 30, bytes_accessed=2 << 20, transcendentals=0
        ),
    )(x, order)
    fold, wave, sib = pl.pallas_call(
        table_kernel,
        out_shape=[
            jax.ShapeDtypeStruct((2 * LOW * GROUP, 2 * SUBS * GROUP), BF),
            jax.ShapeDtypeStruct((LOW, LANES, 2 * LANES), BF),
            jax.ShapeDtypeStruct(x.shape, BF),
        ],
        in_specs=[VM, ANY],
        out_specs=[VM] * 3,
        compiler_params=pltpu.CompilerParams(vmem_limit_bytes=16 << 20),
        cost_estimate=pl.CostEstimate(
            flops=1 << 30, bytes_accessed=2 << 20, transcendentals=0
        ),
    )(sib, own)
    back = moved(again, lambda i: i + 2 if i % 2 == 0 else i - 2)
    *ahead, head, tail = pl.pallas_call(
        forward_kernel,
        out_shape=[jax.ShapeDtypeStruct(x.shape[1:], BF)] * win_dev
        + [
            jax.ShapeDtypeStruct((win_dev, FAR_ROWS, rows, LANES), BF),
            jax.ShapeDtypeStruct((win_dev, ch_dev - FAR_ROWS, rows, LANES), BF),
        ],
        in_specs=[SM, VM, ANY],
        out_specs=[VM] * (win_dev + 2),
        compiler_params=pltpu.CompilerParams(vmem_limit_bytes=16 << 20),
        cost_estimate=pl.CostEstimate(flops=0, bytes_accessed=0, transcendentals=0),
    )(order, ahead, fold)

    def outward(value):
        return moved(value, lambda i: i - 1 if i % 2 == 0 else i + 1)

    head = outward(head)
    tail = lax.cond(jnp.max(named) > FAR_ROWS, outward, jnp.zeros_like, tail)
    near, *back = pl.pallas_call(
        gather_kernel,
        out_shape=[
            jax.ShapeDtypeStruct((win_dev, 5 * ch_dev, rows, LANES), BF),
        ]
        + [jax.ShapeDtypeStruct(x.shape[1:], BF)] * win_dev,
        in_specs=[ANY] * (2 + 2 * win_dev) + [VM, ANY],
        out_specs=[VM] * (1 + win_dev),
        scratch_shapes=[pltpu.SemaphoreType.DMA((win_dev, 4))],
        compiler_params=pltpu.CompilerParams(vmem_limit_bytes=24 << 20),
        cost_estimate=pl.CostEstimate(flops=0, bytes_accessed=0, transcendentals=0),
    )(own, sib, *ahead, *[swap(a) for a in ahead], back, tail)
    late = pl.pallas_call(
        late_kernel,
        out_shape=jax.ShapeDtypeStruct((win_dev, 2 * ch_dev, rows, LANES), BF),
        in_specs=[ANY] * (win_dev + 2),
        out_specs=VM,
        scratch_shapes=[pltpu.SemaphoreType.DMA((win_dev, 3))],
        compiler_params=pltpu.CompilerParams(vmem_limit_bytes=16 << 20),
        cost_estimate=pl.CostEstimate(
            flops=20 << 30, bytes_accessed=0, transcendentals=0
        ),
    )(*[swap(b) for b in back], head, tail)

    ends = lax.dynamic_index_in_dim(pair_ends, me, 0, keepdims=False)
    first = ends[:, 0] % ch_dev
    away = (ends[:, 1] // ch_dev - me) * (1 - 2 * odd)
    row = ends[:, 1] % ch_dev
    mine = lax.dynamic_index_in_dim(place, me, 0, keepdims=False)
    mine = jnp.sum(jnp.where(row[:, None] == channel[None, :], mine[None, :], 0), axis=1)
    row = jnp.where(away == -HALF, mine, row)
    second = jnp.zeros_like(away)
    for n, d in enumerate((0, 1, 2, -1, -2, 3, -3)):
        second = jnp.where(away == d, n * ch_dev + row, second)

    factor = jnp.where(jnp.arange(bins) == 0, 1.0, 2.0).astype(F32)
    weight = (passband * factor).reshape(SUBS, LANES)

    z = lax.axis_index("win")
    give = jax.ShapeDtypeStruct((5, half, wide, slots), BF)
    keep, up, down = pl.pallas_call(
        corr_kernel,
        out_shape=[jax.ShapeDtypeStruct((6, half, wide, slots), F32), give, give],
        in_specs=[SM] * 4 + [VM] * 5,
        out_specs=[VM] * 3,
        scratch_shapes=[
            pltpu.VMEM((2, GROUP * rows, 2 * LANES), BF),
            pltpu.VMEM((LOW, win_dev * slots, 2 * LANES), BF),
            pltpu.VMEM((LOW, LANES, win_dev * slots), F32),
        ],
        compiler_params=pltpu.CompilerParams(vmem_limit_bytes=32 << 20),
        cost_estimate=pl.CostEstimate(
            flops=8 << 30, bytes_accessed=8 << 20, transcendentals=0
        ),
    )(first, second, live_pairs, z.reshape(1), near, late, weight, fold, wave)

    def along(value, step):
        return lax.ppermute(
            value, "win", [(i, (i + step) % win_count) for i in range(win_count)]
        )

    piece = (2, half, wide, slots)
    mine, behind, ahead = pl.pallas_call(
        merge_kernel,
        out_shape=[jax.ShapeDtypeStruct(piece, d) for d in (F32, BF, BF)],
        in_specs=[VM] * 3,
        out_specs=[VM] * 3,
        compiler_params=pltpu.CompilerParams(vmem_limit_bytes=8 << 20),
    )(keep, along(up, 1), along(down, -1))
    return pl.pallas_call(
        final_kernel,
        out_shape=jax.ShapeDtypeStruct((slots, LOW * wide), F32),
        in_specs=[VM] * 3,
        out_specs=VM,
        scratch_shapes=[pltpu.VMEM((LOW * wide, slots), F32)],
        compiler_params=pltpu.CompilerParams(vmem_limit_bytes=8 << 20),
    )(mine, along(behind, -3), along(ahead, 3))


def solution(mesh):
    placed = (P("win", "pair", None, None), P(), P(), P("pair"))
    return jax.shard_map(
        local, mesh=mesh, in_specs=placed, out_specs=P("pair", "win"), check_vma=False
    )
```

```python
import functools
import math

import jax
import jax.numpy as jnp
from jax import lax
from jax.experimental import pallas as pl
from jax.experimental.pallas import tpu as pltpu
from jax.sharding import PartitionSpec as P

HALF = 3
BF = jnp.bfloat16
F32 = jnp.float32
VM = pl.BlockSpec(memory_space=pltpu.VMEM)
SM = pl.BlockSpec(memory_space=pltpu.SMEM)
ANY = pl.BlockSpec(memory_space=pl.ANY)

LANES = 128
SUBS = 16
LOW = 2 * SUBS
FAR_ROWS = 40
GROUP = 8


def moved(value, where):
    count = lax.axis_size("pair")
    pairs = [(i, where(i)) for i in range(count)]
    return lax.ppermute(value, "pair", [(a, b) for a, b in pairs if 0 <= b < count])


def swap(value):
    count = lax.axis_size("pair")
    return lax.ppermute(value, "pair", [(i, i ^ 1) for i in range(count)])


def whiten_into(ref, out_refs, first=0):
    windows, channels, rows, _ = ref.shape
    size = GROUP * rows
    r = lax.broadcasted_iota(jnp.int32, (size, size), 0)
    c = lax.broadcasted_iota(jnp.int32, (size, size), 1)
    source = (r // rows) * rows + 2 * (r % SUBS) + (r // SUBS) % 2
    perm = jnp.where(c == source, 1.0, 0.0).astype(BF)

    for v in range(windows):
        for g in range(channels // GROUP):
            values = ref[v, pl.ds(g * GROUP, GROUP)].astype(F32)
            power = jnp.sum(jnp.sum(values * values, axis=1), axis=1, keepdims=True)
            power = power * (1.0 / (rows * LANES))
            scaled = (values * lax.rsqrt(power + 1e-06)[:, :, None]).astype(BF)
            ordered = jnp.dot(perm, scaled.reshape(size, LANES), preferred_element_type=F32)
            at = pl.ds(first + g * GROUP, GROUP)
            out_refs[v][at] = ordered.astype(BF).reshape(GROUP, rows, LANES)


def windows_of(ref):
    return [ref.at[v] for v in range(ref.shape[0])]


def own_kernel(own_ref, _, again_ref, out_ref):
    again_ref[...] = own_ref[...]
    whiten_into(own_ref, windows_of(out_ref))


def lay(refs, out_ref, sem):
    copies = []
    at = 0
    for n, ref in enumerate(refs):
        copies.append(pltpu.make_async_copy(ref, out_ref.at[pl.ds(at, ref.shape[0])], sem.at[n]))
        copies[-1].start()
        at += ref.shape[0]
    return copies, at


def gather_kernel(own_ref, sib_ref, *refs):
    windows = own_ref.shape[0]
    *in_refs, raw_ref, _, near_ref = refs[: -windows - 1]
    out_refs, sem = refs[-windows - 1 : -1], refs[-1]
    copies = []
    for v in range(windows):
        parts = (own_ref.at[v], sib_ref.at[v], *in_refs[v::windows])
        more, at = lay(parts, near_ref.at[v], sem.at[v])
        copies += more
    whiten_into(raw_ref, out_refs)
    for v in range(windows):
        near_ref[v, pl.ds(at, raw_ref.shape[1])] = out_refs[v][...]
    for copy in copies:
        copy.wait()


def forward_kernel(order_ref, raw_ref, _, *refs):
    *out_refs, head_ref, tail_ref = refs
    whiten_into(raw_ref, out_refs)
    head, tail = head_ref.shape[1], tail_ref.shape[1]
    for v, out_ref in enumerate(out_refs):
        for p in range(head):
            head_ref[v, p] = out_ref[order_ref[p]]
        for p in range(tail):
            tail_ref[v, p] = out_ref[order_ref[head + p]]


def late_kernel(*refs):
    *swapped_refs, head_ref, tail_ref, out_ref, sem = refs
    copies = []
    for v in range(out_ref.shape[0]):
        parts = (swapped_refs[v], head_ref.at[v], tail_ref.at[v])
        copies += lay(parts, out_ref.at[v], sem.at[v])[0]
    for copy in copies:
        copy.wait()


def corr_kernel(
    first_ref,
    second_ref,
    live_ref,
    z_ref,
    near_ref,
    late_ref,
    weight_ref,
    fold_ref,
    wave_ref,
    keep_ref,
    up_ref,
    down_ref,
    cross,
    mid,
    corr,
):
    windows, early = near_ref.shape[:2]
    slots = mid.shape[1] // windows
    weight = weight_ref[...]
    alive = lax.broadcasted_iota(jnp.int32, (1, slots), 1) < live_ref[0]
    _, half_rows, wide, _ = up_ref.shape
    count = LANES // wide

    for v in range(windows):
        for g in range(slots // (2 * GROUP)):
            buf = g % 2
            for half in range(2):
                for q in range(GROUP):
                    p = g * 2 * GROUP + half * GROUP + q
                    a = near_ref[v, first_ref[p]].astype(F32)
                    at = second_ref[p]
                    b = jnp.where(
                        at < early,
                        near_ref[v, jnp.minimum(at, early - 1)],
                        late_ref[v, jnp.maximum(at - early, 0)],
                    ).astype(F32)
                    ar, ai, br, bi = a[:SUBS], a[SUBS:], b[:SUBS], b[SUBS:]
                    re = (ar * br + ai * bi) * weight
                    im = (ai * br - ar * bi) * weight
                    cols = pl.ds(half * LANES, LANES)
                    cross[buf, pl.ds(q * 2 * SUBS, SUBS), cols] = re.astype(BF)
                    cross[buf, pl.ds(q * 2 * SUBS + SUBS, SUBS), cols] = im.astype(BF)
            y = jnp.dot(fold_ref[...], cross[buf], preferred_element_type=F32)
            for part in range(2):
                z = y[part * LOW * GROUP : (part + 1) * LOW * GROUP]
                z = jnp.concatenate(
                    [
                        z[:, :LANES].reshape(LOW, GROUP, LANES),
                        z[:, LANES:].reshape(LOW, GROUP, LANES),
                    ],
                    axis=1,
                )
                rows = pl.ds(v * slots + g * 2 * GROUP, 2 * GROUP)
                mid[:, rows, pl.ds(part * LANES, LANES)] = z.astype(BF)

    def lags(t2, top):
        c = lax.dot_general(
            wave_ref[t2], mid[t2], (((1,), (1,)), ((), ())), preferred_element_type=F32
        )
        corr[t2] = c
        return jnp.maximum(top, jnp.abs(c))

    top = jnp.zeros((LANES, windows * slots), F32)
    top = lax.fori_loop(0, LOW, lags, top, unroll=True)
    peak = jnp.max(top, axis=0, keepdims=True) + 1e-06
    scale = [
        jnp.where(alive, 0.25 / peak[:, v * slots : (v + 1) * slots], 0.0)
        for v in range(windows)
    ]

    jobs = []
    for step, give_ref in ((1, up_ref), (-1, down_ref)):
        jobs += [(step, n, give_ref, n) for n in range(2)]
        jobs += [(-2 * step, n, give_ref, 2 + n) for n in range(2)]
        jobs += [(4, (1 + step) // 2, give_ref, 4)]
    for k, step in enumerate((0, -3, 3)):
        jobs += [(step, n, keep_ref, 2 * k + n) for n in range(2)]
    for step, n, ref, at in jobs:
        rows = pl.ds(lax.rem(z_ref[0] + step + count, count) * wide, wide)

        def emit(t, _, n=n, ref=ref, at=at, rows=rows):
            t2 = t + n * half_rows
            value = corr[t2, rows, pl.ds(0, slots)] * scale[0]
            for v in range(1, windows):
                value = value + corr[t2, rows, pl.ds(v * slots, slots)] * scale[v]
            ref[at, t] = value.astype(ref.dtype)
            return 0

        lax.fori_loop(0, half_rows, emit, 0, unroll=True)


def merge_kernel(keep_ref, left_ref, right_ref, own_ref, behind_ref, ahead_ref):
    for n in range(2):
        own_ref[n] = keep_ref[n] + left_ref[n].astype(F32) + right_ref[n].astype(F32)
        behind = keep_ref[2 + n] + left_ref[2 + n].astype(F32)
        ahead = keep_ref[4 + n] + right_ref[2 + n].astype(F32)
        if n == 0:
            behind = behind + right_ref[4].astype(F32)
        else:
            ahead = ahead + left_ref[4].astype(F32)
        behind_ref[n] = behind.astype(BF)
        ahead_ref[n] = ahead.astype(BF)


def final_kernel(own_ref, *refs):
    *other_refs, out_ref, total = refs
    halves, half_rows, wide, _ = own_ref.shape
    low = halves * half_rows
    for t2 in range(low):
        n, t = divmod(t2, half_rows)
        rows = own_ref[n, t]
        for ref in other_refs:
            rows = rows + ref[n, t].astype(F32)
        total[pl.ds(t2 * wide, wide)] = rows
    group = LANES // low
    for g in range(wide // group):
        rows = [total[pl.ds(g * group + t, low, stride=wide)] for t in range(group)]
        out_ref[:, pl.ds(g * LANES, LANES)] = jnp.concatenate(rows, axis=0).T


def table_kernel(sib_ref, _own, _first, _second, fold_ref, wave_ref, sib_out_ref):
    def turns(rows, cols, period):
        r = lax.broadcasted_iota(jnp.int32, (rows, cols), 0)
        c = lax.broadcasted_iota(jnp.int32, (rows, cols), 1)
        angle = lax.rem(r * c, period).astype(F32) * (2.0 * math.pi / period)
        return jnp.cos(angle), jnp.sin(angle)

    whiten_into(sib_ref, windows_of(sib_out_ref))

    cos, sin = turns(LOW, SUBS, LOW)
    base = jnp.concatenate(
        [jnp.concatenate([cos, -sin], axis=1), jnp.concatenate([sin, cos], axis=1)], axis=0
    ).astype(BF)
    rows, cols = fold_ref.shape
    spread_rows = lax.broadcasted_iota(jnp.int32, (rows, 2 * LOW), 0) // GROUP
    spread_rows = spread_rows == lax.broadcasted_iota(jnp.int32, (rows, 2 * LOW), 1)
    spread_cols = lax.rem(lax.broadcasted_iota(jnp.int32, (2 * SUBS, cols), 1), 2 * SUBS)
    spread_cols = spread_cols == lax.broadcasted_iota(jnp.int32, (2 * SUBS, cols), 0)
    fold = jnp.dot(spread_rows.astype(F32).astype(BF), base, preferred_element_type=F32)
    fold = jnp.dot(
        fold.astype(BF), spread_cols.astype(F32).astype(BF), preferred_element_type=F32
    )
    q_row = lax.rem(lax.broadcasted_iota(jnp.int32, (rows, cols), 0), GROUP)
    q_col = lax.broadcasted_iota(jnp.int32, (rows, cols), 1) // (2 * SUBS)
    fold_ref[...] = jnp.where(q_row == q_col, fold, 0.0).astype(BF)

    low_cos, low_sin = turns(LOW, LANES, LOW * LANES)
    high_cos, high_sin = turns(LANES, LANES, LANES)
    for t2 in range(LOW):
        c, s = low_cos[t2 : t2 + 1], low_sin[t2 : t2 + 1]
        wave_ref[t2, :, pl.ds(0, LANES)] = (c * high_cos - s * high_sin).astype(BF)
        wave_ref[t2, :, pl.ds(LANES, LANES)] = (-s * high_cos - c * high_sin).astype(BF)


def far_order(pair_ends, ch_dev):
    block = jnp.arange(pair_ends.shape[0], dtype=jnp.int32)[:, None]
    away = (pair_ends[:, :, 1] // ch_dev - block) * (1 - 2 * (block % 2))
    named = jnp.where(away == -HALF, pair_ends[:, :, 1] % ch_dev, -1)
    channel = jnp.arange(ch_dev, dtype=jnp.int32)
    need = jnp.any(named[:, :, None] == channel, axis=1)
    count = jnp.sum(need.astype(jnp.int32), axis=1, keepdims=True)
    before = (channel[None, :] < channel[:, None])[None]
    rank = jnp.sum((before & need[:, None, :]).astype(jnp.int32), axis=2)
    return jnp.where(need, rank, count + channel - rank), count


def local(spectra, passband, pair_ends, live_pairs):
    win_count = lax.axis_size("win")
    win_dev, ch_dev, _, bins = spectra.shape
    slots = pair_ends.shape[1]
    rows = 2 * SUBS
    wide = LANES // win_count
    half = LOW // 2
    x = spectra.reshape(win_dev, ch_dev, 2, SUBS, LANES).transpose(0, 1, 3, 2, 4)
    x = x.reshape(win_dev, ch_dev, rows, LANES)
    me = lax.axis_index("pair")
    odd = me % 2
    place, named = far_order(pair_ends, ch_dev)
    target = jnp.clip(me - 1 + 2 * odd, 0, pair_ends.shape[0] - 1)
    channel = jnp.arange(ch_dev, dtype=jnp.int32)
    order = lax.dynamic_index_in_dim(place, target, 0, keepdims=False)
    order = jnp.sum(jnp.where(order[None, :] == channel[:, None], channel[None, :], 0), axis=1)

    ends = lax.dynamic_index_in_dim(pair_ends, me, 0, keepdims=False)
    first = ends[:, 0] % ch_dev
    away = (ends[:, 1] // ch_dev - me) * (1 - 2 * odd)
    row = ends[:, 1] % ch_dev
    mine = lax.dynamic_index_in_dim(place, me, 0, keepdims=False)
    mine = jnp.sum(jnp.where(row[:, None] == channel[None, :], mine[None, :], 0), axis=1)
    row = jnp.where(away == -HALF, mine, row)
    second = jnp.zeros_like(away)
    for n, d in enumerate((0, 1, 2, -1, -2, 3, -3)):
        second = jnp.where(away == d, n * ch_dev + row, second)

    ahead = moved(x, lambda i: i - 2 if i % 2 == 0 else i + 2)
    sib = swap(x)
    again, own = pl.pallas_call(
        own_kernel,
        out_shape=[jax.ShapeDtypeStruct(x.shape, BF)] * 2,
        in_specs=[VM, SM],
        out_specs=[VM] * 2,
        compiler_params=pltpu.CompilerParams(vmem_limit_bytes=16 << 20),
        cost_estimate=pl.CostEstimate(
            flops=1 << 30, bytes_accessed=2 << 20, transcendentals=0
        ),
    )(x, order)
    fold, wave, sib = pl.pallas_call(
        table_kernel,
        out_shape=[
            jax.ShapeDtypeStruct((2 * LOW * GROUP, 2 * SUBS * GROUP), BF),
            jax.ShapeDtypeStruct((LOW, LANES, 2 * LANES), BF),
            jax.ShapeDtypeStruct(x.shape, BF),
        ],
        in_specs=[VM, ANY, SM, SM],
        out_specs=[VM] * 3,
        compiler_params=pltpu.CompilerParams(vmem_limit_bytes=16 << 20),
        cost_estimate=pl.CostEstimate(
            flops=1 << 30, bytes_accessed=2 << 20, transcendentals=0
        ),
    )(sib, own, first, second)
    back = moved(again, lambda i: i + 2 if i % 2 == 0 else i - 2)
    *ahead, head, tail = pl.pallas_call(
        forward_kernel,
        out_shape=[jax.ShapeDtypeStruct(x.shape[1:], BF)] * win_dev
        + [
            jax.ShapeDtypeStruct((win_dev, FAR_ROWS, rows, LANES), BF),
            jax.ShapeDtypeStruct((win_dev, ch_dev - FAR_ROWS, rows, LANES), BF),
        ],
        in_specs=[SM, VM, ANY],
        out_specs=[VM] * (win_dev + 2),
        compiler_params=pltpu.CompilerParams(vmem_limit_bytes=16 << 20),
        cost_estimate=pl.CostEstimate(flops=0, bytes_accessed=0, transcendentals=0),
    )(order, ahead, fold)

    def outward(value):
        return moved(value, lambda i: i - 1 if i % 2 == 0 else i + 1)

    head = outward(head)
    tail = lax.cond(jnp.max(named) > FAR_ROWS, outward, jnp.zeros_like, tail)
    near, *back = pl.pallas_call(
        gather_kernel,
        out_shape=[
            jax.ShapeDtypeStruct((win_dev, 5 * ch_dev, rows, LANES), BF),
        ]
        + [jax.ShapeDtypeStruct(x.shape[1:], BF)] * win_dev,
        in_specs=[ANY] * (2 + 2 * win_dev) + [VM, ANY],
        out_specs=[VM] * (1 + win_dev),
        scratch_shapes=[pltpu.SemaphoreType.DMA((win_dev, 4))],
        compiler_params=pltpu.CompilerParams(vmem_limit_bytes=24 << 20),
        cost_estimate=pl.CostEstimate(flops=0, bytes_accessed=0, transcendentals=0),
    )(own, sib, *ahead, *[swap(a) for a in ahead], back, tail)
    late = pl.pallas_call(
        late_kernel,
        out_shape=jax.ShapeDtypeStruct((win_dev, 2 * ch_dev, rows, LANES), BF),
        in_specs=[ANY] * (win_dev + 2),
        out_specs=VM,
        scratch_shapes=[pltpu.SemaphoreType.DMA((win_dev, 3))],
        compiler_params=pltpu.CompilerParams(vmem_limit_bytes=16 << 20),
        cost_estimate=pl.CostEstimate(
            flops=20 << 30, bytes_accessed=0, transcendentals=0
        ),
    )(*[swap(b) for b in back], head, tail)

    factor = jnp.where(jnp.arange(bins) == 0, 1.0, 2.0).astype(F32)
    weight = (passband * factor).reshape(SUBS, LANES)

    z = lax.axis_index("win")
    give = jax.ShapeDtypeStruct((5, half, wide, slots), BF)
    keep, up, down = pl.pallas_call(
        corr_kernel,
        out_shape=[jax.ShapeDtypeStruct((6, half, wide, slots), F32), give, give],
        in_specs=[SM] * 4 + [VM] * 5,
        out_specs=[VM] * 3,
        scratch_shapes=[
            pltpu.VMEM((2, GROUP * rows, 2 * LANES), BF),
            pltpu.VMEM((LOW, win_dev * slots, 2 * LANES), BF),
            pltpu.VMEM((LOW, LANES, win_dev * slots), F32),
        ],
        compiler_params=pltpu.CompilerParams(vmem_limit_bytes=32 << 20),
        cost_estimate=pl.CostEstimate(
            flops=8 << 30, bytes_accessed=8 << 20, transcendentals=0
        ),
    )(first, second, live_pairs, z.reshape(1), near, late, weight, fold, wave)

    def along(value, step):
        return lax.ppermute(
            value, "win", [(i, (i + step) % win_count) for i in range(win_count)]
        )

    piece = (2, half, wide, slots)
    mine, behind, ahead = pl.pallas_call(
        merge_kernel,
        out_shape=[jax.ShapeDtypeStruct(piece, d) for d in (F32, BF, BF)],
        in_specs=[VM] * 3,
        out_specs=[VM] * 3,
        compiler_params=pltpu.CompilerParams(vmem_limit_bytes=8 << 20),
    )(keep, along(up, 1), along(down, -1))
    return pl.pallas_call(
        final_kernel,
        out_shape=jax.ShapeDtypeStruct((slots, LOW * wide), F32),
        in_specs=[VM] * 3,
        out_specs=VM,
        scratch_shapes=[pltpu.VMEM((LOW * wide, slots), F32)],
        compiler_params=pltpu.CompilerParams(vmem_limit_bytes=8 << 20),
    )(mine, along(behind, -3), along(ahead, 3))


def solution(mesh):
    placed = (P("win", "pair", None, None), P(), P(), P("pair"))
    return jax.shard_map(
        local, mesh=mesh, in_specs=placed, out_specs=P("pair", "win"), check_vma=False
    )
```

```python
import functools
import math

import jax
import jax.numpy as jnp
from jax import lax
from jax.experimental import pallas as pl
from jax.experimental.pallas import tpu as pltpu
from jax.sharding import PartitionSpec as P

HALF = 3
BF = jnp.bfloat16
F32 = jnp.float32
VM = pl.BlockSpec(memory_space=pltpu.VMEM)
SM = pl.BlockSpec(memory_space=pltpu.SMEM)
ANY = pl.BlockSpec(memory_space=pl.ANY)

LANES = 128
SUBS = 16
LOW = 2 * SUBS
FAR_ROWS = 40
GROUP = 8


def moved(value, where):
    count = lax.axis_size("pair")
    pairs = [(i, where(i)) for i in range(count)]
    return lax.ppermute(value, "pair", [(a, b) for a, b in pairs if 0 <= b < count])


def swap(value):
    count = lax.axis_size("pair")
    return lax.ppermute(value, "pair", [(i, i ^ 1) for i in range(count)])


def whiten_into(ref, out_refs, first=0):
    windows, channels, rows, _ = ref.shape
    size = GROUP * rows
    r = lax.broadcasted_iota(jnp.int32, (size, size), 0)
    c = lax.broadcasted_iota(jnp.int32, (size, size), 1)
    source = (r // rows) * rows + 2 * (r % SUBS) + (r // SUBS) % 2
    perm = jnp.where(c == source, 1.0, 0.0).astype(BF)

    for v in range(windows):
        for g in range(channels // GROUP):
            values = ref[v, pl.ds(g * GROUP, GROUP)].astype(F32)
            power = jnp.sum(jnp.sum(values * values, axis=1), axis=1, keepdims=True)
            power = power * (1.0 / (rows * LANES))
            scaled = (values * lax.rsqrt(power + 1e-06)[:, :, None]).astype(BF)
            ordered = jnp.dot(perm, scaled.reshape(size, LANES), preferred_element_type=F32)
            at = pl.ds(first + g * GROUP, GROUP)
            out_refs[v][at] = ordered.astype(BF).reshape(GROUP, rows, LANES)


def windows_of(ref):
    return [ref.at[v] for v in range(ref.shape[0])]


def own_kernel(own_ref, _, again_ref, out_ref):
    again_ref[...] = own_ref[...]
    whiten_into(own_ref, windows_of(out_ref))


def lay(refs, out_ref, sem):
    copies = []
    at = 0
    for n, ref in enumerate(refs):
        copies.append(pltpu.make_async_copy(ref, out_ref.at[pl.ds(at, ref.shape[0])], sem.at[n]))
        copies[-1].start()
        at += ref.shape[0]
    return copies, at


def gather_kernel(own_ref, sib_ref, *refs):
    windows = own_ref.shape[0]
    *in_refs, raw_ref, _, near_ref = refs[: -windows - 1]
    out_refs, sem = refs[-windows - 1 : -1], refs[-1]
    copies = []
    for v in range(windows):
        parts = (own_ref.at[v], sib_ref.at[v], *in_refs[v::windows])
        more, at = lay(parts, near_ref.at[v], sem.at[v])
        copies += more
    whiten_into(raw_ref, out_refs)
    for v in range(windows):
        near_ref[v, pl.ds(at, raw_ref.shape[1])] = out_refs[v][...]
    for copy in copies:
        copy.wait()


def forward_kernel(order_ref, raw_ref, _, *refs):
    *out_refs, head_ref, tail_ref = refs
    whiten_into(raw_ref, out_refs)
    head, tail = head_ref.shape[1], tail_ref.shape[1]
    for v, out_ref in enumerate(out_refs):
        for p in range(head):
            head_ref[v, p] = out_ref[order_ref[p]]
        for p in range(tail):
            tail_ref[v, p] = out_ref[order_ref[head + p]]


def corr_kernel(
    first_ref,
    second_ref,
    live_ref,
    z_ref,
    near_ref,
    swapped_refs,
    head_ref,
    tail_ref,
    weight_ref,
    fold_ref,
    wave_ref,
    keep_ref,
    up_ref,
    down_ref,
    late_ref,
    cross,
    mid,
    corr,
    sem,
):
    copies = []
    for v, ref in enumerate(swapped_refs):
        parts = (ref, head_ref.at[v], tail_ref.at[v])
        copies += lay(parts, late_ref.at[v], sem.at[v])[0]
    for copy in copies:
        copy.wait()
    windows, early = near_ref.shape[:2]
    slots = mid.shape[1] // windows
    weight = weight_ref[...]
    alive = lax.broadcasted_iota(jnp.int32, (1, slots), 1) < live_ref[0]
    _, half_rows, wide, _ = up_ref.shape
    count = LANES // wide

    for v in range(windows):
        for g in range(slots // (2 * GROUP)):
            buf = g % 2
            for half in range(2):
                for q in range(GROUP):
                    p = g * 2 * GROUP + half * GROUP + q
                    a = near_ref[v, first_ref[p]].astype(F32)
                    at = second_ref[p]
                    b = jnp.where(
                        at < early,
                        near_ref[v, jnp.minimum(at, early - 1)],
                        late_ref[v, jnp.maximum(at - early, 0)],
                    ).astype(F32)
                    ar, ai, br, bi = a[:SUBS], a[SUBS:], b[:SUBS], b[SUBS:]
                    re = (ar * br + ai * bi) * weight
                    im = (ai * br - ar * bi) * weight
                    cols = pl.ds(half * LANES, LANES)
                    cross[buf, pl.ds(q * 2 * SUBS, SUBS), cols] = re.astype(BF)
                    cross[buf, pl.ds(q * 2 * SUBS + SUBS, SUBS), cols] = im.astype(BF)
            y = jnp.dot(fold_ref[...], cross[buf], preferred_element_type=F32)
            for part in range(2):
                z = y[part * LOW * GROUP : (part + 1) * LOW * GROUP]
                z = jnp.concatenate(
                    [
                        z[:, :LANES].reshape(LOW, GROUP, LANES),
                        z[:, LANES:].reshape(LOW, GROUP, LANES),
                    ],
                    axis=1,
                )
                rows = pl.ds(v * slots + g * 2 * GROUP, 2 * GROUP)
                mid[:, rows, pl.ds(part * LANES, LANES)] = z.astype(BF)

    def lags(t2, top):
        c = lax.dot_general(
            wave_ref[t2], mid[t2], (((1,), (1,)), ((), ())), preferred_element_type=F32
        )
        corr[t2] = c
        return jnp.maximum(top, jnp.abs(c))

    top = jnp.zeros((LANES, windows * slots), F32)
    top = lax.fori_loop(0, LOW, lags, top, unroll=True)
    peak = jnp.max(top, axis=0, keepdims=True) + 1e-06
    scale = [
        jnp.where(alive, 0.25 / peak[:, v * slots : (v + 1) * slots], 0.0)
        for v in range(windows)
    ]

    jobs = []
    for step, give_ref in ((1, up_ref), (-1, down_ref)):
        jobs += [(step, n, give_ref, n) for n in range(2)]
        jobs += [(-2 * step, n, give_ref, 2 + n) for n in range(2)]
        jobs += [(4, (1 + step) // 2, give_ref, 4)]
    for k, step in enumerate((0, -3, 3)):
        jobs += [(step, n, keep_ref, 2 * k + n) for n in range(2)]
    for step, n, ref, at in jobs:
        rows = pl.ds(lax.rem(z_ref[0] + step + count, count) * wide, wide)

        def emit(t, _, n=n, ref=ref, at=at, rows=rows):
            t2 = t + n * half_rows
            value = corr[t2, rows, pl.ds(0, slots)] * scale[0]
            for v in range(1, windows):
                value = value + corr[t2, rows, pl.ds(v * slots, slots)] * scale[v]
            ref[at, t] = value.astype(ref.dtype)
            return 0

        lax.fori_loop(0, half_rows, emit, 0, unroll=True)


def merge_kernel(keep_ref, left_ref, right_ref, own_ref, behind_ref, ahead_ref):
    for n in range(2):
        own_ref[n] = keep_ref[n] + left_ref[n].astype(F32) + right_ref[n].astype(F32)
        behind = keep_ref[2 + n] + left_ref[2 + n].astype(F32)
        ahead = keep_ref[4 + n] + right_ref[2 + n].astype(F32)
        if n == 0:
            behind = behind + right_ref[4].astype(F32)
        else:
            ahead = ahead + left_ref[4].astype(F32)
        behind_ref[n] = behind.astype(BF)
        ahead_ref[n] = ahead.astype(BF)


def final_kernel(own_ref, *refs):
    *other_refs, out_ref, total = refs
    halves, half_rows, wide, _ = own_ref.shape
    low = halves * half_rows
    for t2 in range(low):
        n, t = divmod(t2, half_rows)
        rows = own_ref[n, t]
        for ref in other_refs:
            rows = rows + ref[n, t].astype(F32)
        total[pl.ds(t2 * wide, wide)] = rows
    group = LANES // low
    for g in range(wide // group):
        rows = [total[pl.ds(g * group + t, low, stride=wide)] for t in range(group)]
        out_ref[:, pl.ds(g * LANES, LANES)] = jnp.concatenate(rows, axis=0).T


def table_kernel(sib_ref, _own, _first, _second, fold_ref, wave_ref, sib_out_ref):
    def turns(rows, cols, period):
        r = lax.broadcasted_iota(jnp.int32, (rows, cols), 0)
        c = lax.broadcasted_iota(jnp.int32, (rows, cols), 1)
        angle = lax.rem(r * c, period).astype(F32) * (2.0 * math.pi / period)
        return jnp.cos(angle), jnp.sin(angle)

    whiten_into(sib_ref, windows_of(sib_out_ref))

    cos, sin = turns(LOW, SUBS, LOW)
    base = jnp.concatenate(
        [jnp.concatenate([cos, -sin], axis=1), jnp.concatenate([sin, cos], axis=1)], axis=0
    ).astype(BF)
    rows, cols = fold_ref.shape
    spread_rows = lax.broadcasted_iota(jnp.int32, (rows, 2 * LOW), 0) // GROUP
    spread_rows = spread_rows == lax.broadcasted_iota(jnp.int32, (rows, 2 * LOW), 1)
    spread_cols = lax.rem(lax.broadcasted_iota(jnp.int32, (2 * SUBS, cols), 1), 2 * SUBS)
    spread_cols = spread_cols == lax.broadcasted_iota(jnp.int32, (2 * SUBS, cols), 0)
    fold = jnp.dot(spread_rows.astype(F32).astype(BF), base, preferred_element_type=F32)
    fold = jnp.dot(
        fold.astype(BF), spread_cols.astype(F32).astype(BF), preferred_element_type=F32
    )
    q_row = lax.rem(lax.broadcasted_iota(jnp.int32, (rows, cols), 0), GROUP)
    q_col = lax.broadcasted_iota(jnp.int32, (rows, cols), 1) // (2 * SUBS)
    fold_ref[...] = jnp.where(q_row == q_col, fold, 0.0).astype(BF)

    low_cos, low_sin = turns(LOW, LANES, LOW * LANES)
    high_cos, high_sin = turns(LANES, LANES, LANES)
    for t2 in range(LOW):
        c, s = low_cos[t2 : t2 + 1], low_sin[t2 : t2 + 1]
        wave_ref[t2, :, pl.ds(0, LANES)] = (c * high_cos - s * high_sin).astype(BF)
        wave_ref[t2, :, pl.ds(LANES, LANES)] = (-s * high_cos - c * high_sin).astype(BF)


def far_order(pair_ends, ch_dev):
    block = jnp.arange(pair_ends.shape[0], dtype=jnp.int32)[:, None]
    away = (pair_ends[:, :, 1] // ch_dev - block) * (1 - 2 * (block % 2))
    named = jnp.where(away == -HALF, pair_ends[:, :, 1] % ch_dev, -1)
    channel = jnp.arange(ch_dev, dtype=jnp.int32)
    need = jnp.any(named[:, :, None] == channel, axis=1)
    count = jnp.sum(need.astype(jnp.int32), axis=1, keepdims=True)
    before = (channel[None, :] < channel[:, None])[None]
    rank = jnp.sum((before & need[:, None, :]).astype(jnp.int32), axis=2)
    return jnp.where(need, rank, count + channel - rank), count


def local(spectra, passband, pair_ends, live_pairs):
    win_count = lax.axis_size("win")
    win_dev, ch_dev, _, bins = spectra.shape
    slots = pair_ends.shape[1]
    rows = 2 * SUBS
    wide = LANES // win_count
    half = LOW // 2
    x = spectra.reshape(win_dev, ch_dev, 2, SUBS, LANES).transpose(0, 1, 3, 2, 4)
    x = x.reshape(win_dev, ch_dev, rows, LANES)
    me = lax.axis_index("pair")
    odd = me % 2
    place, named = far_order(pair_ends, ch_dev)
    target = jnp.clip(me - 1 + 2 * odd, 0, pair_ends.shape[0] - 1)
    channel = jnp.arange(ch_dev, dtype=jnp.int32)
    order = lax.dynamic_index_in_dim(place, target, 0, keepdims=False)
    order = jnp.sum(jnp.where(order[None, :] == channel[:, None], channel[None, :], 0), axis=1)

    ends = lax.dynamic_index_in_dim(pair_ends, me, 0, keepdims=False)
    first = ends[:, 0] % ch_dev
    away = (ends[:, 1] // ch_dev - me) * (1 - 2 * odd)
    row = ends[:, 1] % ch_dev
    mine = lax.dynamic_index_in_dim(place, me, 0, keepdims=False)
    mine = jnp.sum(jnp.where(row[:, None] == channel[None, :], mine[None, :], 0), axis=1)
    row = jnp.where(away == -HALF, mine, row)
    second = jnp.zeros_like(away)
    for n, d in enumerate((0, 1, 2, -1, -2, 3, -3)):
        second = jnp.where(away == d, n * ch_dev + row, second)

    ahead = moved(x, lambda i: i - 2 if i % 2 == 0 else i + 2)
    sib = swap(x)
    again, own = pl.pallas_call(
        own_kernel,
        out_shape=[jax.ShapeDtypeStruct(x.shape, BF)] * 2,
        in_specs=[VM, SM],
        out_specs=[VM] * 2,
        compiler_params=pltpu.CompilerParams(vmem_limit_bytes=16 << 20),
        cost_estimate=pl.CostEstimate(
            flops=1 << 30, bytes_accessed=2 << 20, transcendentals=0
        ),
    )(x, order)
    fold, wave, sib = pl.pallas_call(
        table_kernel,
        out_shape=[
            jax.ShapeDtypeStruct((2 * LOW * GROUP, 2 * SUBS * GROUP), BF),
            jax.ShapeDtypeStruct((LOW, LANES, 2 * LANES), BF),
            jax.ShapeDtypeStruct(x.shape, BF),
        ],
        in_specs=[VM, ANY, SM, SM],
        out_specs=[VM] * 3,
        compiler_params=pltpu.CompilerParams(vmem_limit_bytes=16 << 20),
        cost_estimate=pl.CostEstimate(
            flops=1 << 30, bytes_accessed=2 << 20, transcendentals=0
        ),
    )(sib, own, first, second)
    back = moved(again, lambda i: i + 2 if i % 2 == 0 else i - 2)
    *ahead, head, tail = pl.pallas_call(
        forward_kernel,
        out_shape=[jax.ShapeDtypeStruct(x.shape[1:], BF)] * win_dev
        + [
            jax.ShapeDtypeStruct((win_dev, FAR_ROWS, rows, LANES), BF),
            jax.ShapeDtypeStruct((win_dev, ch_dev - FAR_ROWS, rows, LANES), BF),
        ],
        in_specs=[SM, VM, ANY],
        out_specs=[VM] * (win_dev + 2),
        compiler_params=pltpu.CompilerParams(vmem_limit_bytes=16 << 20),
        cost_estimate=pl.CostEstimate(flops=0, bytes_accessed=0, transcendentals=0),
    )(order, ahead, fold)

    def outward(value):
        return moved(value, lambda i: i - 1 if i % 2 == 0 else i + 1)

    head = outward(head)
    tail = lax.cond(jnp.max(named) > FAR_ROWS, outward, jnp.zeros_like, tail)
    near, *back = pl.pallas_call(
        gather_kernel,
        out_shape=[
            jax.ShapeDtypeStruct((win_dev, 5 * ch_dev, rows, LANES), BF),
        ]
        + [jax.ShapeDtypeStruct(x.shape[1:], BF)] * win_dev,
        in_specs=[ANY] * (2 + 2 * win_dev) + [VM, ANY],
        out_specs=[VM] * (1 + win_dev),
        scratch_shapes=[pltpu.SemaphoreType.DMA((win_dev, 4))],
        compiler_params=pltpu.CompilerParams(vmem_limit_bytes=24 << 20),
        cost_estimate=pl.CostEstimate(flops=0, bytes_accessed=0, transcendentals=0),
    )(own, sib, *ahead, *[swap(a) for a in ahead], back, tail)
    swapped = [swap(b) for b in back]

    factor = jnp.where(jnp.arange(bins) == 0, 1.0, 2.0).astype(F32)
    weight = (passband * factor).reshape(SUBS, LANES)

    z = lax.axis_index("win")
    give = jax.ShapeDtypeStruct((5, half, wide, slots), BF)
    keep, up, down = pl.pallas_call(
        corr_kernel,
        out_shape=[jax.ShapeDtypeStruct((6, half, wide, slots), F32), give, give],
        in_specs=[SM] * 4 + [VM, [ANY] * win_dev, ANY, ANY] + [VM] * 3,
        out_specs=[VM] * 3,
        scratch_shapes=[
            pltpu.VMEM((win_dev, 2 * ch_dev, rows, LANES), BF),
            pltpu.VMEM((2, GROUP * rows, 2 * LANES), BF),
            pltpu.VMEM((LOW, win_dev * slots, 2 * LANES), BF),
            pltpu.VMEM((LOW, LANES, win_dev * slots), F32),
            pltpu.SemaphoreType.DMA((win_dev, 3)),
        ],
        compiler_params=pltpu.CompilerParams(vmem_limit_bytes=32 << 20),
        cost_estimate=pl.CostEstimate(
            flops=8 << 30, bytes_accessed=8 << 20, transcendentals=0
        ),
    )(first, second, live_pairs, z.reshape(1), near, swapped, head, tail, weight, fold, wave)

    def along(value, step):
        return lax.ppermute(
            value, "win", [(i, (i + step) % win_count) for i in range(win_count)]
        )

    piece = (2, half, wide, slots)
    mine, behind, ahead = pl.pallas_call(
        merge_kernel,
        out_shape=[jax.ShapeDtypeStruct(piece, d) for d in (F32, BF, BF)],
        in_specs=[VM] * 3,
        out_specs=[VM] * 3,
        compiler_params=pltpu.CompilerParams(vmem_limit_bytes=8 << 20),
    )(keep, along(up, 1), along(down, -1))
    return pl.pallas_call(
        final_kernel,
        out_shape=jax.ShapeDtypeStruct((slots, LOW * wide), F32),
        in_specs=[VM] * 3,
        out_specs=VM,
        scratch_shapes=[pltpu.VMEM((LOW * wide, slots), F32)],
        compiler_params=pltpu.CompilerParams(vmem_limit_bytes=8 << 20),
    )(mine, along(behind, -3), along(ahead, 3))


def solution(mesh):
    placed = (P("win", "pair", None, None), P(), P(), P("pair"))
    return jax.shard_map(
        local, mesh=mesh, in_specs=placed, out_specs=P("pair", "win"), check_vma=False
    )
```
